128 devices in a mesh: lon: 8 (over y, x_hi), lat: 16 (over x_lo, z, core).
Axes of the slice: x: 4 (x_hi: 2, x_lo: 2; x = x_hi * 2 + x_lo), y: 4, z: 4, core: 2. Of those that a mesh axis runs over, the one named last changes fastest.
Arguments:
- field: float32 [80, 4096, 2048], P(None, 'lon', 'lat'), may hold values from -6 to 6
- lon_test: float32 [4096, 200], P('lon'), may hold values from -0.09375 to 0.09375
- lat_test: float32 [2048, 200], P('lat'), may hold values from -0.125 to 0.125
- time_test: float32 [80, 200], replicated, may hold values from -0.625 to 0.625
- lon_core: float32 [96, 4096], P(None, 'lon'), may hold values from -0.09375 to 0.09375
- lat_core: float32 [96, 2048], P(None, 'lat'), may hold values from -0.125 to 0.125
- time_core: float32 [96, 80], replicated, may hold values from -0.625 to 0.625
Outputs:
- sketch_lon: float32 [4096, 200], P(('lon', 'lat'))
- sketch_lat: float32 [2048, 200], P('lat')
- sketch_time: float32 [80, 200], replicated
- core_sketch: float32 [96, 96, 96], P(None, 'lon', 'lat')
The draws below stay inside these ranges and needn't reach their ends.
All inputs are finite; a program needn't handle non-finite values.
Results may differ from the reference program's by a relative error of at most 0.000096.
Values sent between devices are 32-bit elements; how exact they have to be, the bound alone decides.
No kernel may reach another device: no remote copies, remote signals or barrier semaphores. Data moves between devices by JAX's collectives and lax.ppermute only.
A program may use at most 128 MiB of HBM per device.

```python
import jax
import jax.numpy as jnp
from jax import lax

NT = 80
KS = 200
CS = 96
NLON = 4096
NLAT = 2048


def steps_of(stream_key, dims, shards, smallest, high):
    factor_of = 1.0
    for axis_at, blocks in shards:
        draws = jax.random.uniform(jax.random.fold_in(jax.random.fold_in(stream_key, 6), axis_at), (blocks,), jnp.float32, smallest / len(shards), high / len(shards))
        factor_of = factor_of * jnp.repeat(jnp.exp(draws), dims[axis_at] // blocks).reshape((-1,) + (1,) * (len(dims) - 1 - axis_at))
    return factor_of


def centred(stream_key, dims, deviation, reach, split=(), held_as=jnp.bfloat16):
    level = steps_of(stream_key, dims, split, -0.22, 0.18) if split else 1.0
    values = jax.random.normal(stream_key, dims, jnp.float32) * deviation * level
    return jnp.minimum(jnp.maximum(values, -reach), reach).astype(held_as)


def setup_inputs(seed: int = 0) -> dict:
    seeds = jax.random.split(jax.random.key(seed), 8)
    field = centred(seeds[0], (NT, NLON, NLAT), 1.0, 6.0, ((1, 8), (2, 16)), jnp.float32)
    lon_test = centred(seeds[1], (NLON, KS), NLON ** -0.5, 0.09375, ((0, 8),), jnp.float32)
    lat_test = centred(seeds[2], (NLAT, KS), NLAT ** -0.5, 0.125, ((0, 16),), jnp.float32)
    time_test = centred(seeds[3], (NT, KS), NT ** -0.5, 0.625, (), jnp.float32)
    lon_core = centred(seeds[4], (CS, NLON), NLON ** -0.5, 0.09375, ((1, 8),), jnp.float32)
    lat_core = centred(seeds[5], (CS, NLAT), NLAT ** -0.5, 0.125, ((1, 16),), jnp.float32)
    time_core = centred(seeds[6], (CS, NT), NT ** -0.5, 0.625, (), jnp.float32)
    return {"field": field, "lon_test": lon_test, "lat_test": lat_test, "time_test": time_test, "lon_core": lon_core, "lat_core": lat_core, "time_core": time_core}


def reference(field, lon_test, lat_test, time_test, lon_core, lat_core, time_core):
    highest = lax.Precision.HIGHEST
    mixed = jnp.einsum('tij,jk->tik', field, lat_test, precision=highest)
    sketch_lon = jnp.einsum('tik,tk->ik', mixed, time_test, precision=highest)
    sketch_time = jnp.einsum('tik,ik->tk', mixed, lon_test, precision=highest)
    across = jnp.einsum('tij,ik->tkj', field, lon_test, precision=highest)
    sketch_lat = jnp.einsum('tkj,tk->jk', across, time_test, precision=highest)
    narrowed = jnp.einsum('tij,bj->tib', field, lat_core, precision=highest)
    crossed = jnp.einsum('tib,ai->tab', narrowed, lon_core, precision=highest)
    core_sketch = jnp.einsum('tab,ct->cab', crossed, time_core, precision=highest)
    return sketch_lon, sketch_lat, sketch_time, core_sketch
```

```python
import jax
import jax.numpy as jnp
from jax import lax
from jax.experimental import pallas as pl
from jax.experimental.pallas import tpu as pltpu
from jax.sharding import PartitionSpec as P

F32 = jnp.float32
BF16 = jnp.bfloat16
BOTH = ("lon", "lat")
HOURS = 8
VMEM = 56 * 1024 * 1024


def halves(value):
    top = value.astype(BF16)
    return top, (value - top.astype(F32)).astype(BF16)


def dot(left, right, dims=((1,), (0,))):
    return lax.dot_general(left, right, (dims, ((), ())), preferred_element_type=F32)


def stacked_dot(weights, rows, right_top, right_low):
    upper = dot(weights[...], right_top)
    return upper[:rows] + upper[rows:] + dot(weights[:rows], right_low)


def pair_of_hours(field_ref, at):
    return jnp.concatenate([field_ref[at], field_ref[at + 1]], axis=1)


def core_kernel(field_ref, lon_ref, lat_ref, keep_ref, send_ref, weights, crossed):
    step = pl.program_id(0)
    modes = lon_ref.shape[0]

    @pl.when(step == 0)
    def _():
        top, low = halves(lon_ref[...])
        weights[:modes] = top
        weights[modes:] = low

    for at in range(0, HOURS, 2):
        top, low = halves(pair_of_hours(field_ref, at))
        both = stacked_dot(weights, modes, top, low)
        crossed[:, step, at, :] = both[:, :128]
        crossed[:, step, at + 1, :] = both[:, 128:]

    @pl.when(step == pl.num_programs(0) - 1)
    def _():
        lat_top, lat_low = halves(lat_ref[...])
        lats = jnp.concatenate([lat_top, lat_low], axis=0)
        for owner in range(8):
            block = crossed[owner * 12 : owner * 12 + 12].reshape(960, 128)
            block = jnp.concatenate([block, jnp.zeros((64, 128), F32)], axis=0)
            top, low = halves(block)
            upper = dot(lats, top, ((1,), (1,)))
            result = upper[:96] + upper[96:] + dot(lat_top, low, ((1,), (1,)))
            for part, out in enumerate((keep_ref, send_ref)):
                for b in range(6):
                    row = part * 48 + b * 8
                    for q in range(8):
                        out[owner, :, q * 6 + b, :] = result[row : row + 8, q * 128 : q * 128 + 128]


def core_partial(field, lon_core, lat_rows):
    hours, lons, lats = field.shape
    modes = lon_core.shape[0]
    shape = jax.ShapeDtypeStruct((8, 8, 48, 128), F32)
    whole = pl.BlockSpec((8, 8, 48, 128), lambda s: (0, 0, 0, 0))
    return pl.pallas_call(
        core_kernel,
        grid=(hours // HOURS,),
        in_specs=[
            pl.BlockSpec((HOURS, lons, lats), lambda s: (s, 0, 0)),
            pl.BlockSpec((modes, lons), lambda s: (0, 0)),
            pl.BlockSpec((96, lats), lambda s: (0, 0)),
        ],
        out_specs=[whole, whole],
        out_shape=[shape, shape],
        scratch_shapes=[
            pltpu.VMEM((2 * modes, lons), BF16),
            pltpu.VMEM((modes, hours // HOURS, HOURS, lats), F32),
        ],
        compiler_params=pltpu.CompilerParams(vmem_limit_bytes=VMEM),
        cost_estimate=pl.CostEstimate(flops=6 * hours * lons * lats * modes, bytes_accessed=24 << 20, transcendentals=0),
        name="core_partial",
    )(field, lon_core, lat_rows)


def across_kernel(field_ref, lon_ref, lat_ref, time_ref, out_ref, weights, lat_t):
    step = pl.program_id(0)
    rank = lat_t.shape[0]

    @pl.when(step == 0)
    def _():
        top, low = halves(lon_ref[...].T)
        weights[:rank] = top
        weights[rank:] = low
        lat_t[...] = lat_ref[...].T
        out_ref[...] = jnp.zeros_like(out_ref)

    times = time_ref[...].T
    lane = lax.broadcasted_iota(jnp.int32, (rank, 128), 1)
    lat_sum = out_ref[0]
    hour_sum = out_ref[1]
    for at in range(0, HOURS, 2):
        top, low = halves(pair_of_hours(field_ref, at))
        both = stacked_dot(weights, rank, top, low)
        for part in range(2):
            across = both[:, part * 128 : part * 128 + 128]
            hour = at + part
            lat_sum = lat_sum + across * times[:, hour : hour + 1]
            total = jnp.sum(across * lat_t[...], axis=1, keepdims=True)
            hour_sum = jnp.where(lane == step * HOURS + hour, total, hour_sum)
    out_ref[0] = lat_sum
    out_ref[1] = hour_sum


def across_partial(field, lon_test, lat_test, time_test):
    hours, lons, lats = field.shape
    rank = lon_test.shape[1]
    return pl.pallas_call(
        across_kernel,
        grid=(hours // HOURS,),
        in_specs=[
            pl.BlockSpec((HOURS, lons, lats), lambda s: (s, 0, 0)),
            pl.BlockSpec((lons, rank), lambda s: (0, 0)),
            pl.BlockSpec((lats, rank), lambda s: (0, 0)),
            pl.BlockSpec((HOURS, rank), lambda s: (s, 0)),
        ],
        out_specs=pl.BlockSpec((2, rank, 128), lambda s: (0, 0, 0)),
        out_shape=jax.ShapeDtypeStruct((2, rank, 128), F32),
        scratch_shapes=[pltpu.VMEM((2 * rank, lons), BF16), pltpu.VMEM((rank, lats), F32)],
        compiler_params=pltpu.CompilerParams(vmem_limit_bytes=VMEM),
        cost_estimate=pl.CostEstimate(flops=6 * hours * lons * lats * rank, bytes_accessed=22 << 20, transcendentals=0),
        name="across_partial",
    )(field, lon_test, lat_test, time_test)


def lon_kernel(field_ref, lat_ref, time_ref, out_ref):
    @pl.when(pl.program_id(0) == 0)
    def _():
        out_ref[...] = jnp.zeros_like(out_ref)

    total = out_ref[...]
    for at in range(0, HOURS, 2):
        top, low = halves(pair_of_hours(field_ref, at))
        tests = [lat_ref[...] * time_ref[hour : hour + 1, :] for hour in (at, at + 1)]
        test_top, test_low = halves(jnp.concatenate(tests, axis=0))
        total = total + dot(top, test_top) + dot(low, test_top) + dot(top, test_low)
    out_ref[...] = total


def lon_partial(field, lat_test, time_test):
    hours, lons, lats = field.shape
    rank = lat_test.shape[1]
    return pl.pallas_call(
        lon_kernel,
        grid=(hours // HOURS,),
        in_specs=[
            pl.BlockSpec((HOURS, lons, lats), lambda s: (s, 0, 0)),
            pl.BlockSpec((lats, rank), lambda s: (0, 0)),
            pl.BlockSpec((HOURS, rank), lambda s: (s, 0)),
        ],
        out_specs=pl.BlockSpec((lons, rank), lambda s: (0, 0)),
        out_shape=jax.ShapeDtypeStruct((lons, rank), F32),
        compiler_params=pltpu.CompilerParams(vmem_limit_bytes=VMEM),
        cost_estimate=pl.CostEstimate(flops=6 * hours * lons * lats * rank, bytes_accessed=22 << 20, transcendentals=0),
        name="lon_partial",
    )(field, lat_test, time_test)


def finish_kernel(parts_ref, time_ref, out_ref):
    total = parts_ref[0]
    for source in range(1, parts_ref.shape[0]):
        total = total + parts_ref[source]
    flipped = total.T
    column = jnp.concatenate([flipped[:, q * 6 : q * 6 + 6] for q in range(8)], axis=0)
    for a in range(12):
        out_ref[:, a, :] = lax.dot_general(
            time_ref[...],
            column[a * 80 : a * 80 + 80],
            (((1,), (0,)), ((), ())),
            precision=lax.Precision.HIGHEST,
            preferred_element_type=F32,
        )


def finish_core(parts, time_core):
    return pl.pallas_call(
        finish_kernel,
        out_shape=jax.ShapeDtypeStruct((96, 12, 6), F32),
        compiler_params=pltpu.CompilerParams(vmem_limit_bytes=VMEM),
        name="finish_core",
    )(parts, time_core)


def places(move):
    pairs = []
    for source in range(128):
        lon, lat = divmod(source, 16)
        x, y, z, core = (lon % 2) * 2 + lat // 8, lon // 2, lat // 2 % 4, lat % 2
        x, y, z, core = move(x, y, z, core)
        pairs.append((source, (y * 2 + x // 2) * 16 + x % 2 * 8 + z * 2 + core))
    return pairs


OTHER_CORE = places(lambda x, y, z, core: (x, y, z, 1 - core))
Y_FLIP = places(lambda x, y, z, core: (x, y ^ 1, z, core))
Y_FOLD = places(lambda x, y, z, core: (x, 3 - y, z, core))
Z_FLIP = places(lambda x, y, z, core: (x, y, z ^ 1, core))
Z_FOLD = places(lambda x, y, z, core: (x, y, 3 - z, core))
X_FLIP = places(lambda x, y, z, core: (x ^ 1, y, z, core))
X_HALF = places(lambda x, y, z, core: (x ^ 2, y, z, core))
SAME_CORE = [[lon * 16 + 2 * at + core for lon in range(8) for at in range(8)] for core in (0, 1)]


def add_from(value, pairs):
    return value + lax.ppermute(value, BOTH, pairs)


def on_device(field, lon_test, lat_test, time_test, lon_core, lat_core, time_core):
    core = lax.axis_index("lat") % 2

    rows = lat_core.reshape(8, 2, 6, -1)
    rows = jnp.where(core == 0, rows, rows[:, ::-1])
    rows = rows.transpose(1, 2, 0, 3).reshape(96, -1)
    keep, send = core_partial(field, lon_core, rows)
    arrived = lax.ppermute(send, BOTH, OTHER_CORE)
    chip = (keep + arrived).reshape(64, 48, 128)
    parts = lax.all_to_all(chip, BOTH, 0, 0, axis_index_groups=SAME_CORE)

    sums = across_partial(field, lon_test, lat_test, time_test)
    other = lax.ppermute(lax.dynamic_slice(sums[1], ((1 - core) * 96, 0), (104, 128)), BOTH, OTHER_CORE)
    hour = lax.dynamic_slice(sums[1], (core * 96, 0), (104, 128)) + other
    joined = jnp.concatenate([sums[0], hour], axis=0)
    for pairs in (Y_FLIP, Y_FOLD, X_HALF):
        joined = add_from(joined, pairs)
    sketch_lat = joined[:200].T
    hour = joined[200:]
    for pairs in (Z_FLIP, Z_FOLD, X_FLIP):
        hour = add_from(hour, pairs)
    other = lax.ppermute(hour, BOTH, OTHER_CORE)
    first, second = jnp.where(core == 0, hour, other), jnp.where(core == 0, other, hour)
    sketch_time = jnp.concatenate([first[:96], second], axis=0).T[:80]

    lon_part = lon_partial(field, lat_test, time_test)
    shares = lax.all_to_all(lon_part.reshape(16, 32, 200), "lat", 0, 0)
    sketch_lon = jnp.sum(shares, axis=0)

    core_sketch = finish_core(parts, time_core)
    return (sketch_lon, sketch_lat, sketch_time, core_sketch)


def solution(mesh):
    return jax.shard_map(
        on_device,
        mesh=mesh,
        in_specs=(
            P(None, "lon", "lat"),
            P("lon", None),
            P("lat", None),
            P(),
            P(None, "lon"),
            P(None, "lat"),
            P(),
        ),
        out_specs=(P(("lon", "lat"), None), P("lat", None), P(), P(None, "lon", "lat")),
        check_vma=False,
    )
```

```python
import jax
import jax.numpy as jnp
from jax import lax
from jax.experimental import pallas as pl
from jax.experimental.pallas import tpu as pltpu
from jax.sharding import PartitionSpec as P

F32 = jnp.float32
BF16 = jnp.bfloat16
BOTH = ("lon", "lat")
HOURS = 8
VMEM = 48 * 1024 * 1024
MOST_VMEM = 62 * 1024 * 1024
SLOTS = (
    22, 12, 52, 3, 19, 5, 60, 58, 2, 33, 10, 8, 29, 26, 25, 9,
    44, 18, 62, 11, 47, 40, 15, 39, 56, 57, 32, 23, 49, 43, 21, 45,
    42, 34, 35, 46, 20, 61, 37, 14, 63, 53, 0, 38, 27, 50, 1, 55,
    6, 13, 24, 41, 30, 28, 59, 31, 7, 16, 4, 48, 51, 54, 36, 17,
)


def halves(value):
    top = value.astype(BF16)
    return top, (value - top.astype(F32)).astype(BF16)


def dot(left, right, dims=((1,), (0,))):
    return lax.dot_general(left, right, (dims, ((), ())), preferred_element_type=F32)


def stacked_dot(weights, rows, right_top, right_low):
    upper = dot(weights[...], right_top)
    return upper[:rows] + upper[rows:] + dot(weights[:rows], right_low)


def block_copy(field_hbm, field, arrived, at):
    part = pl.ds(at * HOURS, HOURS)
    return pltpu.make_async_copy(field_hbm.at[part], field.at[part], arrived.at[at])


def start_field(field_hbm, field, arrived, blocks):
    for at in blocks:
        block_copy(field_hbm, field, arrived, at).start()


def each_block(field_hbm, field, arrived, work):
    def step(at, carry):
        block_copy(field_hbm, field, arrived, at).wait()
        work(at)
        return carry

    lax.fori_loop(0, arrived.shape[0], step, 0)


def field_scratch(hours, lons, lats):
    return [pltpu.VMEM((hours, lons, lats), F32), pltpu.SemaphoreType.DMA((hours // HOURS,))]


def copies_in(sources, targets, arrived):
    copies = [pltpu.make_async_copy(a, b, arrived.at[i]) for i, (a, b) in enumerate(zip(sources, targets))]
    for copy in copies:
        copy.start()
    return copies


def in_vmem(count):
    return [pl.BlockSpec(memory_space=pltpu.VMEM)] * count


def in_hbm(count):
    return [pl.BlockSpec(memory_space=pltpu.HBM)] * count


def first_kernel(
    field_hbm, lon_core_hbm, lon_test_hbm, lat_test_hbm, time_hbm, lat_core_hbm, send_hbm, keep_hbm, sums_ref,
    field, arrived, lon_core, lon_test, lat_test, time_test, lat_core, small, weights, crossed, lat_sum, hour_sum,
    shares, sent,
):
    modes, rank = lon_core.shape[0], lon_test.shape[0]
    rows = modes + rank
    lane = lax.broadcasted_iota(jnp.int32, (rank, 128), 1)
    sources = (lon_core_hbm, lon_test_hbm, lat_test_hbm, time_hbm, lat_core_hbm)
    waits = copies_in(sources, (lon_core, lon_test, lat_test, time_test, lat_core), small)
    start_field(field_hbm, field, arrived, range(1))
    lat_sum[...] = jnp.zeros_like(lat_sum)
    hour_sum[...] = jnp.zeros_like(hour_sum)
    for copy in waits:
        copy.wait()
    start_field(field_hbm, field, arrived, range(1, arrived.shape[0]))
    top, low = halves(jnp.concatenate([lon_core[...], lon_test[...]], axis=0))
    weights[:rows] = top
    weights[rows:] = low

    def work(at):
        times = time_test[pl.ds(at * HOURS, HOURS), :].T
        lat_total, hour_total = lat_sum[...], hour_sum[...]
        for pair in range(0, HOURS, 2):
            first = at * HOURS + pair
            top, low = halves(jnp.concatenate([field[first], field[first + 1]], axis=1))
            both = stacked_dot(weights, rows, top, low)
            for part in range(2):
                hour = pair + part
                result = both[:, part * 128 : part * 128 + 128]
                crossed[:, at, hour, :] = result[:modes]
                across = result[modes:]
                lat_total = lat_total + across * times[:, hour : hour + 1]
                total = jnp.sum(across * lat_test[...], axis=1, keepdims=True)
                hour_total = jnp.where(lane == at * HOURS + hour, total, hour_total)
        lat_sum[...] = lat_total
        hour_sum[...] = hour_total

    each_block(field_hbm, field, arrived, work)

    core = lax.axis_index("lat") % 2
    of_core = [
        jnp.concatenate([lat_core[pl.ds(at * 6 + b, 8, stride=12), :] for b in range(6)], axis=0) for at in range(2)
    ]
    lat_rows = jnp.concatenate(
        [jnp.where(core == 0, of_core[0], of_core[1]), jnp.where(core == 0, of_core[1], of_core[0])], axis=0
    )
    lat_top, lat_low = halves(lat_rows)
    lats = jnp.concatenate(
        [jnp.concatenate([lat_top, lat_top], axis=1), jnp.concatenate([lat_low, jnp.zeros_like(lat_low)], axis=1)],
        axis=0,
    )

    def share_copies(owner):
        targets = ((1, send_hbm), (0, keep_hbm))
        return [pltpu.make_async_copy(shares.at[p, owner], out.at[owner], sent.at[p, owner]) for p, out in targets]

    def share(owner, carry):
        block = crossed[pl.ds(owner * 12, 12)].reshape(960, 128)
        block = jnp.concatenate([block, jnp.zeros((64, 128), F32)], axis=0)
        result = dot(lats, jnp.concatenate(halves(block), axis=1), ((1,), (1,)))
        result = result[:96] + result[96:]
        for part in (1, 0):
            for b in range(6):
                row = part * 48 + b * 8
                for q in range(8):
                    shares[part, owner, :, q * 6 + b, :] = result[row : row + 8, q * 128 : q * 128 + 128]
        for copy in share_copies(owner):
            copy.start()
        return carry

    lax.fori_loop(0, 8, share, 0)
    for group in range(25):
        for part, total in enumerate((lat_sum, hour_sum)):
            tile = total[group * 8 : group * 8 + 8]
            sums_ref[2 * group, part * 4 : part * 4 + 4] = tile[:4]
            sums_ref[2 * group + 1, part * 4 : part * 4 + 4] = tile[4:]
    sums_ref[50:] = jnp.zeros((14, 8, 128), F32)
    for owner in range(8):
        for copy in share_copies(owner):
            copy.wait()


def first_partials(field, lon_core, lon_test_t, lat_test_t, time_test, lat_core):
    hours, lons, lats = field.shape
    modes, rank = lon_core.shape[0], lon_test_t.shape[0]
    part = jax.ShapeDtypeStruct((8, 8, 48, 128), F32)
    return pl.pallas_call(
        first_kernel,
        in_specs=in_hbm(6),
        out_specs=in_hbm(2) + in_vmem(1),
        out_shape=[part, part, jax.ShapeDtypeStruct((64, 8, 128), F32)],
        scratch_shapes=field_scratch(hours, lons, lats)
        + [pltpu.VMEM(x.shape, F32) for x in (lon_core, lon_test_t, lat_test_t, time_test, lat_core)]
        + [
            pltpu.SemaphoreType.DMA((5,)),
            pltpu.VMEM((2 * (modes + rank), lons), BF16),
            pltpu.VMEM((modes, hours // HOURS, HOURS, lats), F32),
            pltpu.VMEM((rank, 128), F32),
            pltpu.VMEM((rank, 128), F32),
            pltpu.VMEM((2, 8, 8, 48, 128), F32),
            pltpu.SemaphoreType.DMA((2, 8)),
        ],
        compiler_params=pltpu.CompilerParams(vmem_limit_bytes=MOST_VMEM),
        cost_estimate=pl.CostEstimate(flops=20 * 10**9, bytes_accessed=28 << 20, transcendentals=0),
        name="first_partials",
    )(field, lon_core, lon_test_t, lat_test_t, time_test, lat_core)


def join_kernel(keep_hbm, arrived_hbm, sums_hbm, out_hbm, keep, arrived, sums, copied, out, sent):
    pieces = [pl.ds(at * 16, 16) for at in range(4)]
    waits = copies_in(
        [sums_hbm] + [ref.at[piece] for piece in pieces for ref in (keep_hbm, arrived_hbm)],
        [sums] + [ref.at[piece] for piece in pieces for ref in (keep, arrived)],
        copied,
    )
    waits[0].wait()
    for at in range(4):
        waits[1 + 2 * at].wait()
        waits[2 + 2 * at].wait()
        for chip in range(at * 16, at * 16 + 16):
            slot = SLOTS.index(chip)
            out[slot, :48] = keep[chip] + arrived[chip]
            out[slot, 48:] = sums[chip % 8]
    copies = []
    for at, piece in enumerate(pieces):
        copies.append(pltpu.make_async_copy(out.at[piece], out_hbm.at[piece], sent.at[at]))
        copies[-1].start()
    for copy in copies:
        copy.wait()


def join_shares(keep, arrived, sums):
    shape = (64, 56, 128)
    return pl.pallas_call(
        join_kernel,
        in_specs=[pl.BlockSpec(memory_space=pl.ANY)] * 3,
        out_specs=pl.BlockSpec(memory_space=pl.ANY),
        out_shape=jax.ShapeDtypeStruct(shape, F32),
        scratch_shapes=[pltpu.VMEM(x.shape, F32) for x in (keep, arrived, sums)]
        + [pltpu.SemaphoreType.DMA((9,)), pltpu.VMEM(shape, F32), pltpu.SemaphoreType.DMA((4,))],
        compiler_params=pltpu.CompilerParams(vmem_limit_bytes=MOST_VMEM),
        cost_estimate=pl.CostEstimate(flops=10**6, bytes_accessed=5 << 20, transcendentals=0),
        name="join_shares",
    )(keep, arrived, sums)


def lon_kernel(field_hbm, lat_ref, time_ref, keep_ref, send_ref, field, arrived, lat_test, total):
    start_field(field_hbm, field, arrived, range(arrived.shape[0]))
    total[...] = jnp.zeros_like(total)
    lat_test[...] = lat_ref[...].T
    lons = total.shape[0]

    def work(at):
        times = time_ref[pl.ds(at * HOURS, HOURS), :]
        tests = [lat_test[...] * times[hour : hour + 1, :] for hour in range(HOURS)]
        test_top, test_low = halves(jnp.concatenate(tests, axis=0))
        values = [halves(field[at * HOURS + hour]) for hour in range(HOURS)]
        top = jnp.concatenate([value[0] for value in values], axis=1)
        low = jnp.concatenate([value[1] for value in values], axis=1)
        upper = dot(jnp.concatenate([top, low], axis=0), test_top)
        total[...] += upper[:lons] + upper[lons:] + dot(top, test_low)

    each_block(field_hbm, field, arrived, work)
    place = lax.axis_index("lat")
    core, z, x_lo = place % 2, place // 2 % 4, place // 8
    for at in range(8):
        flip, step = at // 4, at % 4
        x = x_lo + flip - 2 * x_lo * flip
        owner = x * 8 + (z + step) % 4 * 2
        for out, of_core in ((keep_ref, core), (send_ref, 1 - core)):
            out[at] = total[pl.ds(pl.multiple_of((owner + of_core) * 32, 32), 32), :]


def lon_partial(field, lat_test_t, time_test):
    hours, lons, lats = field.shape
    rank = lat_test_t.shape[0]
    out = jax.ShapeDtypeStruct((8, 32, rank), F32)
    return pl.pallas_call(
        lon_kernel,
        in_specs=in_hbm(1) + in_vmem(2),
        out_specs=in_vmem(2),
        out_shape=[out, out],
        scratch_shapes=field_scratch(hours, lons, lats)
        + [pltpu.VMEM((lats, rank), F32), pltpu.VMEM((lons, rank), F32)],
        compiler_params=pltpu.CompilerParams(vmem_limit_bytes=VMEM),
        cost_estimate=pl.CostEstimate(flops=12 * 10**9, bytes_accessed=22 << 20, transcendentals=0),
        name="lon_partial",
    )(field, lat_test_t, time_test)


def finish_kernel(parts_ref, time_ref, core_ref, lat_ref, time_out_ref, columns):
    total = parts_ref[0, :48]
    for source in range(1, parts_ref.shape[0]):
        total = total + parts_ref[source, :48]
    modes = [jnp.concatenate([total[q * 6 : q * 6 + 6], jnp.zeros((2, 128), F32)], axis=0) for q in range(8)]
    modes = jnp.concatenate(modes, axis=1)
    rows = jnp.concatenate([modes[:, a * 80 : a * 80 + 80] for a in range(12)], axis=0)
    result = lax.dot_general(
        rows,
        time_ref[...],
        (((1,), (0,)), ((), ())),
        precision=lax.Precision.HIGHEST,
        preferred_element_type=F32,
    )
    for a in range(12):
        core_ref[a] = result[a * 8 : a * 8 + 6]
    for slot, chip in enumerate(SLOTS):
        if chip < 50:
            lat_ref[chip * 4 : chip * 4 + 4] = parts_ref[slot, 48:52]
            columns[chip * 4 : chip * 4 + 4] = parts_ref[slot, 52:]
    time_out_ref[...] = columns[...].T[:80]


def finish(parts, time_core_t):
    return pl.pallas_call(
        finish_kernel,
        out_shape=[
            jax.ShapeDtypeStruct((12, 6, 96), F32),
            jax.ShapeDtypeStruct((200, 128), F32),
            jax.ShapeDtypeStruct((80, 200), F32),
        ],
        scratch_shapes=[pltpu.VMEM((200, 128), F32)],
        compiler_params=pltpu.CompilerParams(vmem_limit_bytes=VMEM),
        cost_estimate=pl.CostEstimate(flops=10**8, bytes_accessed=2 << 20, transcendentals=0),
        name="finish",
    )(parts, time_core_t)


def places(move):
    pairs = []
    for source in range(128):
        lon, lat = divmod(source, 16)
        x, y, z, core = (lon % 2) * 2 + lat // 8, lon // 2, lat // 2 % 4, lat % 2
        x, y, z, core = move(x, y, z, core)
        pairs.append((source, (y * 2 + x // 2) * 16 + x % 2 * 8 + z * 2 + core))
    return pairs


OTHER_CORE = places(lambda x, y, z, core: (x, y, z, 1 - core))
CHIPS = [[lon * 16 + 2 * at + core for lon in range(8) for at in range(8)] for core in (0, 1)]
MIXED = [[chips[chip] for chip in SLOTS] for chips in CHIPS]


def on_device(field, lon_test, lat_test, time_test, lon_core, lat_core, time_core):
    send, keep, sums = first_partials(field, lon_core, lon_test.T, lat_test.T, time_test, lat_core)
    other = lax.ppermute(send, BOTH, OTHER_CORE)

    shares = lax.all_to_all(sums, BOTH, 0, 0, axis_index_groups=CHIPS)
    by_lat = jnp.sum(shares.reshape(8, 8, 8, 128), axis=0)
    by_hour = jnp.sum(by_lat, axis=0)
    by_hour = by_hour + lax.ppermute(by_hour, BOTH, OTHER_CORE)
    is_lat = lax.broadcasted_iota(jnp.int32, (8, 8, 128), 1) < 4
    sums = jnp.where(is_lat, by_lat, by_hour)

    chip = join_shares(keep.reshape(64, 48, 128), other.reshape(64, 48, 128), sums)
    parts = lax.all_to_all(chip, BOTH, 0, 0, axis_index_groups=MIXED)

    field, _ = lax.optimization_barrier((field, chip))
    keep, send = lon_partial(field, lat_test.T, time_test)
    shares = keep + lax.ppermute(send, BOTH, OTHER_CORE)
    sketch_lon = shares[0]
    for at in range(1, 8):
        pairs = places(lambda x, y, z, core: (x ^ (at // 4), y, (z + at) % 4, core))
        sketch_lon = sketch_lon + lax.ppermute(shares[at], BOTH, pairs)

    core_sketch, sketch_lat, sketch_time = finish(parts, time_core.T)
    return (sketch_lon, sketch_lat.T, sketch_time, core_sketch.transpose(2, 0, 1))


def solution(mesh):
    return jax.shard_map(
        on_device,
        mesh=mesh,
        in_specs=(
            P(None, "lon", "lat"),
            P("lon", None),
            P("lat", None),
            P(),
            P(None, "lon"),
            P(None, "lat"),
            P(),
        ),
        out_specs=(P(("lon", "lat"), None), P("lat", None), P(), P(None, "lon", "lat")),
        check_vma=False,
    )
```

```python
import jax
import jax.numpy as jnp
from jax import lax
from jax.experimental import pallas as pl
from jax.experimental.pallas import tpu as pltpu
from jax.sharding import PartitionSpec as P

F32 = jnp.float32
BF16 = jnp.bfloat16
BOTH = ("lon", "lat")
HOURS = 8
VMEM = 48 * 1024 * 1024
MOST_VMEM = 62 * 1024 * 1024
MUCH_VMEM = 40 * 1024 * 1024
SLOTS = sorted(range(64), key=lambda chip: (chip % 4, chip // 16, chip // 8 % 2 * 2 + chip // 4 % 2))


def halves(value):
    top = value.astype(BF16)
    return top, (value - top.astype(F32)).astype(BF16)


def dot(left, right, dims=((1,), (0,))):
    return lax.dot_general(left, right, (dims, ((), ())), preferred_element_type=F32)


def stacked_dot(weights, rows, right_top, right_low):
    upper = dot(weights[...], right_top)
    return upper[:rows] + upper[rows:] + dot(weights[:rows], right_low)


def block_copy(field_hbm, field, arrived, at):
    part = pl.ds(at * HOURS, HOURS)
    return pltpu.make_async_copy(field_hbm.at[part], field.at[part], arrived.at[at])


def start_field(field_hbm, field, arrived, blocks):
    for at in blocks:
        block_copy(field_hbm, field, arrived, at).start()


def each_block(field_hbm, field, arrived, work):
    def step(at, carry):
        block_copy(field_hbm, field, arrived, at).wait()
        work(at)
        return carry

    lax.fori_loop(0, arrived.shape[0], step, 0)


def field_scratch(hours, lons, lats):
    return [pltpu.VMEM((hours, lons, lats), F32), pltpu.SemaphoreType.DMA((hours // HOURS,))]


def copies_in(sources, targets, arrived):
    copies = [pltpu.make_async_copy(a, b, arrived.at[i]) for i, (a, b) in enumerate(zip(sources, targets))]
    for copy in copies:
        copy.start()
    return copies


def in_vmem(count):
    return [pl.BlockSpec(memory_space=pltpu.VMEM)] * count


def in_hbm(count):
    return [pl.BlockSpec(memory_space=pltpu.HBM)] * count


def split_rows(values, weights):
    rows = values.shape[0]
    top, low = halves(values)
    weights[:rows] = top
    weights[rows:] = low


def products(weights, top, low):
    both = stacked_dot(weights, weights.shape[0] // 2, top, low)
    return both[:, :128], both[:, 128:]


def sketch_kernel(
    field_hbm, lon_hbm, lat_hbm, time_hbm, sums_ref,
    field, arrived, lon_test, lat_test_t, time_test, small, weights, lat_test, lat_sum, hour_sum, lon_sum,
):
    rank, lons = lon_test.shape
    lane = lax.broadcasted_iota(jnp.int32, (rank, 128), 1)
    waits = copies_in((lon_hbm, lat_hbm, time_hbm), (lon_test, lat_test_t, time_test), small)
    start_field(field_hbm, field, arrived, range(1))
    for total in (lat_sum, hour_sum, lon_sum):
        total[...] = jnp.zeros_like(total)
    for copy in waits:
        copy.wait()
    start_field(field_hbm, field, arrived, range(1, arrived.shape[0]))
    split_rows(lon_test[...], weights)
    lat_test[...] = lat_test_t[...].T

    def work(at):
        times = time_test[pl.ds(at * HOURS, HOURS), :]
        times_t = times.T
        lat_total, hour_total = lat_sum[...], hour_sum[...]
        values = [halves(field[at * HOURS + hour]) for hour in range(HOURS)]

        for pair in range(0, HOURS, 2):
            top, low = (jnp.concatenate([values[pair][i], values[pair + 1][i]], axis=1) for i in range(2))
            for hour, across in enumerate(products(weights, top, low), pair):
                lat_total = lat_total + across * times_t[:, hour : hour + 1]
                total = jnp.sum(across * lat_test_t[...], axis=1, keepdims=True)
                hour_total = jnp.where(lane == at * HOURS + hour, total, hour_total)
        lat_sum[...] = lat_total
        hour_sum[...] = hour_total

        tests = [lat_test[...] * times[hour : hour + 1, :] for hour in range(HOURS)]
        test_top, test_low = halves(jnp.concatenate(tests, axis=0))
        top = jnp.concatenate([value[0] for value in values], axis=1)
        low = jnp.concatenate([value[1] for value in values], axis=1)
        upper = dot(jnp.concatenate([top, low], axis=0), test_top)
        lon_sum[...] += upper[:lons] + upper[lons:] + dot(top, test_low)

    each_block(field_hbm, field, arrived, work)
    lon_t = lon_sum[...].T
    for place in range(rank // 2):
        columns = slice(place * 2, place * 2 + 2)
        sums_ref[place, 0, :2] = lat_sum[columns]
        sums_ref[place, 0, 2:] = hour_sum[columns]
        for part in range(4):
            row = part % 2 * 2
            sums_ref[place, 1 + part // 2, row : row + 2] = lon_t[columns, part * 128 : part * 128 + 128]
    sums_ref[rank // 2 :] = jnp.zeros((128 - rank // 2, 3, 4, 128), F32)


def sketch_partials(field, lon_test_t, lat_test_t, time_test):
    hours, lons, lats = field.shape
    rank = lon_test_t.shape[0]
    return pl.pallas_call(
        sketch_kernel,
        in_specs=in_hbm(4),
        out_specs=pl.BlockSpec(memory_space=pltpu.VMEM),
        out_shape=jax.ShapeDtypeStruct((128, 3, 4, 128), F32),
        scratch_shapes=field_scratch(hours, lons, lats)
        + [pltpu.VMEM(x.shape, F32) for x in (lon_test_t, lat_test_t, time_test)]
        + [
            pltpu.SemaphoreType.DMA((3,)),
            pltpu.VMEM((2 * rank, lons), BF16),
            pltpu.VMEM((lats, rank), F32),
            pltpu.VMEM((rank, 128), F32),
            pltpu.VMEM((rank, 128), F32),
            pltpu.VMEM((lons, rank), F32),
        ],
        compiler_params=pltpu.CompilerParams(vmem_limit_bytes=MOST_VMEM),
        cost_estimate=pl.CostEstimate(flops=24 * 10**9, bytes_accessed=22 << 20, transcendentals=0),
        name="sketch_partials",
    )(field, lon_test_t, lat_test_t, time_test)


def sum_kernel(shares_ref, keep_ref, send_ref):
    core = lax.axis_index("lat") % 2
    mine = lax.broadcasted_iota(jnp.int32, (4, 128), 0) // 2 == core

    def spread(rows):
        return jnp.where(mine, jnp.concatenate([rows, rows], axis=0), 0.0)

    hour = jnp.zeros((4, 128), F32)
    for at in range(8):
        lats = []
        for lat in (at * 2, at * 2 + 1):
            total = shares_ref[lat, 0]
            for lon in range(1, 8):
                total = total + shares_ref[lon * 16 + lat, 0]
            hour = hour + total
            lats.append(spread(total[:2]))
        tile, row = 17 + at // 2, at % 2 * 4
        keep_ref[tile, row : row + 4] = jnp.where(core == 0, lats[0], lats[1])
        send_ref[tile, row : row + 4] = jnp.where(core == 0, lats[1], lats[0])
    hour = spread(hour[2:])
    for out in (keep_ref, send_ref):
        out[16, :4] = hour
        out[16, 4:] = hour
    for lon in range(8):
        for half in range(2):
            total = shares_ref[lon * 16, 1 + half]
            for lat in range(1, 16):
                total = total + shares_ref[lon * 16 + lat, 1 + half]
            for out in (keep_ref, send_ref):
                out[lon * 2 + half, :4] = spread(total[:2])
                out[lon * 2 + half, 4:] = spread(total[2:])


def sum_shares(shares):
    return pl.pallas_call(
        sum_kernel,
        out_shape=[jax.ShapeDtypeStruct((21, 8, 128), F32)] * 2,
        compiler_params=pltpu.CompilerParams(vmem_limit_bytes=MUCH_VMEM),
        cost_estimate=pl.CostEstimate(flops=10**6, bytes_accessed=1 << 20, transcendentals=0),
        name="sum_shares",
    )(shares)


def core_kernel(
    field_hbm, lon_core, lat_core, send_ref, keep_ref, field, arrived, weights, crossed
):
    start_field(field_hbm, field, arrived, range(arrived.shape[0]))
    split_rows(lon_core[...], weights)

    def work(at):
        for pair in range(0, HOURS, 2):
            first = at * HOURS + pair
            top, low = halves(jnp.concatenate([field[first], field[first + 1]], axis=1))
            for hour, result in enumerate(products(weights, top, low), pair):
                crossed[:, at, hour, :] = result

    each_block(field_hbm, field, arrived, work)

    core = lax.axis_index("lat") % 2
    of_core = [
        jnp.concatenate([lat_core[pl.ds(at * 6 + b, 8, stride=12), :] for b in range(6)], axis=0) for at in range(2)
    ]
    lat_rows = jnp.concatenate(
        [jnp.where(core == 0, of_core[0], of_core[1]), jnp.where(core == 0, of_core[1], of_core[0])], axis=0
    )
    lat_top, lat_low = halves(lat_rows)
    lats = jnp.concatenate(
        [jnp.concatenate([lat_top, lat_top], axis=1), jnp.concatenate([lat_low, jnp.zeros_like(lat_low)], axis=1)],
        axis=0,
    )

    def share(owner, carry):
        block = crossed[pl.ds(owner * 12, 12)].reshape(960, 128)
        block = jnp.concatenate([block, jnp.zeros((64, 128), F32)], axis=0)
        result = dot(lats, jnp.concatenate(halves(block), axis=1), ((1,), (1,)))
        result = result[:96] + result[96:]
        for part, out in enumerate((keep_ref, send_ref)):
            for b in range(6):
                row = part * 48 + b * 8
                for q in range(8):
                    out[owner, :, q * 6 + b, :] = result[row : row + 8, q * 128 : q * 128 + 128]
        return carry

    lax.fori_loop(0, 8, share, 0)


def core_partials(field, lon_core, lat_core):
    hours, lons, lats = field.shape
    modes = lon_core.shape[0]
    part = jax.ShapeDtypeStruct((8, 8, 48, 128), F32)
    return pl.pallas_call(
        core_kernel,
        in_specs=in_hbm(1) + in_vmem(2),
        out_specs=in_vmem(2),
        out_shape=[part, part],
        scratch_shapes=field_scratch(hours, lons, lats)
        + [
            pltpu.VMEM((2 * modes, lons), BF16),
            pltpu.VMEM((modes, hours // HOURS, HOURS, lats), F32),
        ],
        compiler_params=pltpu.CompilerParams(vmem_limit_bytes=MUCH_VMEM),
        cost_estimate=pl.CostEstimate(flops=30 * 10**9, bytes_accessed=28 << 20, transcendentals=0),
        name="core_partials",
    )(field, lon_core, lat_core)


def join_kernel(keep_ref, arrived_ref, mine_ref, other_ref, out_ref, rolled, lats):
    core = lax.axis_index("lat") % 2
    rest = (mine_ref[...] + other_ref[...]).reshape(21 * 8, 128)
    hour = rest[16 * 8 : 16 * 8 + 4]
    lats[...] = rest[17 * 8 :]
    for odd in range(2):
        rolled[odd] = jnp.where(core == 0, *[pltpu.roll(rest[:128], (96 - 64 * odd - 32 * c) % 128, 1) for c in range(2)])
    lane = lax.broadcasted_iota(jnp.int32, (4, 128), 1)
    for slot, chip in enumerate(SLOTS):
        lon, lat = divmod(chip, 8)
        out_ref[slot, :48] = keep_ref[chip] + arrived_ref[chip]
        out_ref[slot, 48:52] = lats[lat * 4 : lat * 4 + 4]
        row = lon * 16 + lat // 2 * 4
        out_ref[slot, 52:] = jnp.where(lane < 96, hour, rolled[lat % 2, row : row + 4])


def join_shares(keep, arrived, mine, other):
    shape = (64, 56, 128)
    return pl.pallas_call(
        join_kernel,
        in_specs=in_vmem(4),
        out_specs=pl.BlockSpec(memory_space=pltpu.VMEM),
        out_shape=jax.ShapeDtypeStruct(shape, F32),
        scratch_shapes=[pltpu.VMEM((2, 128, 128), F32), pltpu.VMEM((32, 128), F32)],
        compiler_params=pltpu.CompilerParams(vmem_limit_bytes=MUCH_VMEM),
        cost_estimate=pl.CostEstimate(flops=10**6, bytes_accessed=5 << 20, transcendentals=0),
        name="join_shares",
    )(keep, arrived, mine, other)


def finish_kernel(parts_ref, time_ref, core_ref, lat_ref, hour_ref, lon_ref, columns):
    total = parts_ref[0, :48]
    for source in range(1, parts_ref.shape[0]):
        total = total + parts_ref[source, :48]
    modes = [jnp.concatenate([total[q * 6 : q * 6 + 6], jnp.zeros((2, 128), F32)], axis=0) for q in range(8)]
    modes = jnp.concatenate(modes, axis=1)
    rows = jnp.concatenate([modes[:, a * 80 : a * 80 + 80] for a in range(12)], axis=0)
    result = lax.dot_general(
        rows,
        time_ref[...],
        (((1,), (0,)), ((), ())),
        precision=lax.Precision.HIGHEST,
        preferred_element_type=F32,
    )
    for a in range(12):
        core_ref[a] = result[a * 8 : a * 8 + 6]
    for slot, chip in enumerate(SLOTS):
        if chip < 50:
            lat_ref[chip * 4 : chip * 4 + 4] = parts_ref[slot, 48:52]
            columns[chip * 4 : chip * 4 + 4] = parts_ref[slot, 52:]
    rows = columns[...].T
    hour_ref[...] = rows[:80]
    lon_ref[...] = rows[96:]


def finish(parts, time_core_t):
    return pl.pallas_call(
        finish_kernel,
        out_shape=[
            jax.ShapeDtypeStruct((12, 6, 96), F32),
            jax.ShapeDtypeStruct((200, 128), F32),
            jax.ShapeDtypeStruct((80, 200), F32),
            jax.ShapeDtypeStruct((32, 200), F32),
        ],
        scratch_shapes=[pltpu.VMEM((200, 128), F32)],
        compiler_params=pltpu.CompilerParams(vmem_limit_bytes=VMEM),
        cost_estimate=pl.CostEstimate(flops=10**8, bytes_accessed=2 << 20, transcendentals=0),
        name="finish",
    )(parts, time_core_t)


def places(move):
    pairs = []
    for source in range(128):
        lon, lat = divmod(source, 16)
        x, y, z, core = (lon % 2) * 2 + lat // 8, lon // 2, lat // 2 % 4, lat % 2
        x, y, z, core = move(x, y, z, core)
        pairs.append((source, (y * 2 + x // 2) * 16 + x % 2 * 8 + z * 2 + core))
    return pairs


OTHER_CORE = places(lambda x, y, z, core: (x, y, z, 1 - core))
CHIPS = [[lon * 16 + 2 * at + core for lon in range(8) for at in range(8)] for core in (0, 1)]
MIXED = [[chips[chip] for chip in SLOTS] for chips in CHIPS]


def on_device(field, lon_test, lat_test, time_test, lon_core, lat_core, time_core):
    sums = sketch_partials(field, lon_test.T, lat_test.T, time_test)

    core_field, sums = lax.optimization_barrier((field, sums))
    shares = lax.all_to_all(sums, BOTH, 0, 0)
    send, keep = core_partials(core_field, lon_core, lat_core)
    shares, send, keep = lax.optimization_barrier((shares, send, keep))
    other = lax.ppermute(send, BOTH, OTHER_CORE)
    mine, others = sum_shares(shares)
    others = lax.ppermute(others, BOTH, OTHER_CORE)

    chip = join_shares(keep.reshape(64, 48, 128), other.reshape(64, 48, 128), mine, others)
    parts = lax.all_to_all(chip, BOTH, 0, 0, axis_index_groups=MIXED)
    core_sketch, sketch_lat, sketch_time, sketch_lon = finish(parts, time_core.T)
    return (sketch_lon, sketch_lat.T, sketch_time, core_sketch.transpose(2, 0, 1))


def solution(mesh):
    return jax.shard_map(
        on_device,
        mesh=mesh,
        in_specs=(
            P(None, "lon", "lat"),
            P("lon", None),
            P("lat", None),
            P(),
            P(None, "lon"),
            P(None, "lat"),
            P(),
        ),
        out_specs=(P(("lon", "lat"), None), P("lat", None), P(), P(None, "lon", "lat")),
        check_vma=False,
    )
```

```python
import jax
import jax.numpy as jnp
from jax import lax
from jax.experimental import pallas as pl
from jax.experimental.pallas import tpu as pltpu
from jax.sharding import PartitionSpec as P

F32 = jnp.float32
BF16 = jnp.bfloat16
BOTH = ("lon", "lat")
HOURS = 16
VMEM = 48 * 1024 * 1024
MOST_VMEM = 62 * 1024 * 1024
MUCH_VMEM = 40 * 1024 * 1024
SLOTS = sorted(range(64), key=lambda chip: (chip % 4, chip // 16, chip // 8 % 2 * 2 + chip // 4 % 2))


def halves(value):
    top = value.astype(BF16)
    return top, (value - top.astype(F32)).astype(BF16)


def dot(left, right, dims=((1,), (0,))):
    return lax.dot_general(left, right, (dims, ((), ())), preferred_element_type=F32)


def stacked_dot(weights, rows, right_top, right_low):
    upper = dot(weights[...], right_top)
    return upper[:rows] + upper[rows:] + dot(weights[:rows], right_low)


def block_copy(field_hbm, field, arrived, at):
    part = pl.ds(at * HOURS, HOURS)
    return pltpu.make_async_copy(field_hbm.at[part], field.at[part], arrived.at[at])


def start_field(field_hbm, field, arrived, blocks):
    for at in blocks:
        block_copy(field_hbm, field, arrived, at).start()


def each_block(field_hbm, field, arrived, work):
    def step(at, carry):
        block_copy(field_hbm, field, arrived, at).wait()
        work(at)
        return carry

    lax.fori_loop(0, arrived.shape[0], step, 0)


def field_scratch(hours, lons, lats):
    return [pltpu.VMEM((hours, lons, lats), F32), pltpu.SemaphoreType.DMA((hours // HOURS,))]


def copies_in(sources, targets, arrived):
    copies = [pltpu.make_async_copy(a, b, arrived.at[i]) for i, (a, b) in enumerate(zip(sources, targets))]
    for copy in copies:
        copy.start()
    return copies


def in_vmem(count):
    return [pl.BlockSpec(memory_space=pltpu.VMEM)] * count


def in_hbm(count):
    return [pl.BlockSpec(memory_space=pltpu.HBM)] * count


def split_rows(values, weights):
    rows = values.shape[0]
    top, low = halves(values)
    weights[:rows] = top
    weights[rows:] = low


def products(weights, top, low):
    both = stacked_dot(weights, weights.shape[0] // 2, top, low)
    return both[:, :128], both[:, 128:]


def first_kernel(
    field_hbm, modes_hbm, lon_hbm, lat_hbm, time_hbm, crossed_hbm, sums_ref,
    field, arrived, lon_core, lon_test, lat_test, time_test, small, weights, crossed, sent, lat_sum, hour_sum,
):
    modes, rank = lon_core.shape[0], lon_test.shape[0]
    lane = lax.broadcasted_iota(jnp.int32, (rank, 128), 1)
    waits = copies_in((modes_hbm, lon_hbm, lat_hbm, time_hbm), (lon_core, lon_test, lat_test, time_test), small)
    start_field(field_hbm, field, arrived, range(1))
    for total in (lat_sum, hour_sum):
        total[...] = jnp.zeros_like(total)
    for copy in waits:
        copy.wait()
    start_field(field_hbm, field, arrived, range(1, arrived.shape[0]))
    split_rows(jnp.concatenate([lon_core[...], lon_test[...]], axis=0), weights)

    def crossed_copy(at):
        return pltpu.make_async_copy(crossed.at[:, at], crossed_hbm.at[:, at], sent.at[at])

    def work(at):
        times = time_test[pl.ds(at * HOURS, HOURS), :].T
        lat_total, hour_total = lat_sum[...], hour_sum[...]
        for pair in range(0, HOURS, 2):
            first = at * HOURS + pair
            top, low = halves(jnp.concatenate([field[first], field[first + 1]], axis=1))
            for hour, result in enumerate(products(weights, top, low), pair):
                crossed[:, at, hour, :] = result[:modes]
                across = result[modes:]
                lat_total = lat_total + across * times[:, hour : hour + 1]
                total = jnp.sum(across * lat_test[...], axis=1, keepdims=True)
                hour_total = jnp.where(lane == at * HOURS + hour, total, hour_total)
        lat_sum[...] = lat_total
        hour_sum[...] = hour_total
        crossed_copy(at).start()

    each_block(field_hbm, field, arrived, work)
    for place in range(rank // 2):
        columns = slice(place * 2, place * 2 + 2)
        sums_ref[place, 0, :2] = lat_sum[columns]
        sums_ref[place, 0, 2:] = hour_sum[columns]
    sums_ref[rank // 2 :] = jnp.zeros((128 - rank // 2, 1, 4, 128), F32)
    for at in range(arrived.shape[0]):
        crossed_copy(at).wait()


def first_partials(field, lon_core, lon_test_t, lat_test_t, time_test):
    hours, lons, lats = field.shape
    modes, rank = lon_core.shape[0], lon_test_t.shape[0]
    blocks = hours // HOURS
    crossed = (modes, blocks, HOURS, lats)
    return pl.pallas_call(
        first_kernel,
        in_specs=in_hbm(5),
        out_specs=[pl.BlockSpec(memory_space=pl.ANY)] + in_vmem(1),
        out_shape=[jax.ShapeDtypeStruct(crossed, F32), jax.ShapeDtypeStruct((128, 1, 4, 128), F32)],
        scratch_shapes=field_scratch(hours, lons, lats)
        + [pltpu.VMEM(x.shape, F32) for x in (lon_core, lon_test_t, lat_test_t, time_test)]
        + [
            pltpu.SemaphoreType.DMA((4,)),
            pltpu.VMEM((2 * (modes + rank), lons), BF16),
            pltpu.VMEM(crossed, F32),
            pltpu.SemaphoreType.DMA((blocks,)),
            pltpu.VMEM((rank, 128), F32),
            pltpu.VMEM((rank, 128), F32),
        ],
        compiler_params=pltpu.CompilerParams(vmem_limit_bytes=MOST_VMEM),
        cost_estimate=pl.CostEstimate(flops=18 * 10**9, bytes_accessed=26 << 20, transcendentals=0),
        name="first_partials",
    )(field, lon_core, lon_test_t, lat_test_t, time_test)


def sum_kernel(shares_ref, keep_ref, send_ref):
    core = lax.axis_index("lat") % 2
    mine = lax.broadcasted_iota(jnp.int32, (4, 128), 0) // 2 == core

    def spread(rows):
        return jnp.where(mine, jnp.concatenate([rows, rows], axis=0), 0.0)

    hour = jnp.zeros((4, 128), F32)
    for at in range(8):
        lats = []
        for lat in (at * 2, at * 2 + 1):
            total = shares_ref[lat, 0]
            for lon in range(1, 8):
                total = total + shares_ref[lon * 16 + lat, 0]
            hour = hour + total
            lats.append(spread(total[:2]))
        tile, row = at // 2, at % 2 * 4
        keep_ref[tile, row : row + 4] = jnp.where(core == 0, lats[0], lats[1])
        send_ref[tile, row : row + 4] = jnp.where(core == 0, lats[1], lats[0])
    hour = spread(hour[2:])
    for out in (keep_ref, send_ref):
        out[4, :4] = hour
        out[4, 4:] = hour


def sum_shares(shares):
    return pl.pallas_call(
        sum_kernel,
        out_shape=[jax.ShapeDtypeStruct((5, 8, 128), F32)] * 2,
        compiler_params=pltpu.CompilerParams(vmem_limit_bytes=MUCH_VMEM),
        cost_estimate=pl.CostEstimate(flops=10**6, bytes_accessed=1 << 20, transcendentals=0),
        name="sum_shares",
    )(shares)


def core_kernel(crossed, lat_core, send_ref, keep_ref):
    core = lax.axis_index("lat") % 2
    of_core = [
        jnp.concatenate([lat_core[pl.ds(at * 6 + b, 8, stride=12), :] for b in range(6)], axis=0) for at in range(2)
    ]
    lat_rows = jnp.concatenate(
        [jnp.where(core == 0, of_core[0], of_core[1]), jnp.where(core == 0, of_core[1], of_core[0])], axis=0
    )
    lat_top, lat_low = halves(lat_rows)
    lats = jnp.concatenate(
        [jnp.concatenate([lat_top, lat_top], axis=1), jnp.concatenate([lat_low, jnp.zeros_like(lat_low)], axis=1)],
        axis=0,
    )

    def share(owner, carry):
        block = crossed[pl.ds(owner * 12, 12)].reshape(960, 128)
        block = jnp.concatenate([block, jnp.zeros((64, 128), F32)], axis=0)
        result = dot(lats, jnp.concatenate(halves(block), axis=1), ((1,), (1,)))
        result = result[:96] + result[96:]
        for part, out in enumerate((keep_ref, send_ref)):
            for b in range(6):
                row = part * 48 + b * 8
                for q in range(8):
                    out[owner, :, q * 6 + b, :] = result[row : row + 8, q * 128 : q * 128 + 128]
        return carry

    lax.fori_loop(0, 8, share, 0)


def core_partials(crossed, lat_core):
    part = jax.ShapeDtypeStruct((8, 8, 48, 128), F32)
    return pl.pallas_call(
        core_kernel,
        in_specs=in_vmem(2),
        out_specs=in_vmem(2),
        out_shape=[part, part],
        compiler_params=pltpu.CompilerParams(vmem_limit_bytes=MUCH_VMEM),
        cost_estimate=pl.CostEstimate(flops=20 * 10**9, bytes_accessed=8 << 20, transcendentals=0),
        name="core_partials",
    )(crossed, lat_core)


def join_kernel(keep_ref, arrived_ref, mine_ref, other_ref, out_ref, sums):
    sums[...] = mine_ref[...] + other_ref[...]
    for slot, chip in enumerate(SLOTS):
        lat = chip % 8
        row = lat % 2 * 4
        out_ref[slot, :48] = keep_ref[chip] + arrived_ref[chip]
        out_ref[slot, 48:52] = sums[lat // 2, row : row + 4]
        out_ref[slot, 52:] = sums[4, :4]


def join_shares(keep, arrived, mine, other):
    return pl.pallas_call(
        join_kernel,
        in_specs=in_vmem(4),
        out_specs=pl.BlockSpec(memory_space=pltpu.VMEM),
        out_shape=jax.ShapeDtypeStruct((64, 56, 128), F32),
        scratch_shapes=[pltpu.VMEM(mine.shape, F32)],
        compiler_params=pltpu.CompilerParams(vmem_limit_bytes=MUCH_VMEM),
        cost_estimate=pl.CostEstimate(flops=10**6, bytes_accessed=5 << 20, transcendentals=0),
        name="join_shares",
    )(keep, arrived, mine, other)


def lon_kernel(field_hbm, lat_ref, time_ref, keep_ref, send_ref, field, arrived, lat_test, total):
    start_field(field_hbm, field, arrived, range(arrived.shape[0]))
    total[...] = jnp.zeros_like(total)
    lat_test[...] = lat_ref[...].T
    lons = total.shape[0]

    def work(at):
        times = time_ref[pl.ds(at * HOURS, HOURS), :]
        tests = [lat_test[...] * times[hour : hour + 1, :] for hour in range(HOURS)]
        test_top, test_low = halves(jnp.concatenate(tests, axis=0))
        values = [halves(field[at * HOURS + hour]) for hour in range(HOURS)]
        top = jnp.concatenate([value[0] for value in values], axis=1)
        low = jnp.concatenate([value[1] for value in values], axis=1)
        upper = dot(jnp.concatenate([top, low], axis=0), test_top)
        total[...] += upper[:lons] + upper[lons:] + dot(top, test_low)

    each_block(field_hbm, field, arrived, work)
    place = lax.axis_index("lat")
    core, z, x_lo = place % 2, place // 2 % 4, place // 8
    for step in range(4):
        for flip in range(2):
            x = x_lo + flip - 2 * x_lo * flip
            owner = x * 8 + (z + step) % 4 * 2
            for out, of_core in ((keep_ref, core), (send_ref, 1 - core)):
                out[step, flip] = total[pl.ds(pl.multiple_of((owner + of_core) * 32, 32), 32), :]


def lon_partial(field, lat_test_t, time_test):
    hours, lons, lats = field.shape
    rank = lat_test_t.shape[0]
    out = jax.ShapeDtypeStruct((4, 2, 32, rank), F32)
    return pl.pallas_call(
        lon_kernel,
        in_specs=in_hbm(1) + in_vmem(2),
        out_specs=in_vmem(2),
        out_shape=[out, out],
        scratch_shapes=field_scratch(hours, lons, lats)
        + [pltpu.VMEM((lats, rank), F32), pltpu.VMEM((lons, rank), F32)],
        compiler_params=pltpu.CompilerParams(vmem_limit_bytes=MUCH_VMEM),
        cost_estimate=pl.CostEstimate(flops=12 * 10**9, bytes_accessed=22 << 20, transcendentals=0),
        name="lon_partial",
    )(field, lat_test_t, time_test)


def finish_kernel(parts_ref, time_ref, core_ref, lat_ref, hour_ref, columns):
    total = parts_ref[0, :48]
    for source in range(1, parts_ref.shape[0]):
        total = total + parts_ref[source, :48]
    modes = [jnp.concatenate([total[q * 6 : q * 6 + 6], jnp.zeros((2, 128), F32)], axis=0) for q in range(8)]
    modes = jnp.concatenate(modes, axis=1)
    rows = jnp.concatenate([modes[:, a * 80 : a * 80 + 80] for a in range(12)], axis=0)
    result = lax.dot_general(
        rows,
        time_ref[...],
        (((1,), (0,)), ((), ())),
        precision=lax.Precision.HIGHEST,
        preferred_element_type=F32,
    )
    for a in range(12):
        core_ref[a] = result[a * 8 : a * 8 + 6]
    for slot, chip in enumerate(SLOTS):
        if chip < 50:
            lat_ref[chip * 4 : chip * 4 + 4] = parts_ref[slot, 48:52]
            columns[chip * 4 : chip * 4 + 4] = parts_ref[slot, 52:]
    hour_ref[...] = columns[...].T[:80]


def finish(parts, time_core_t):
    return pl.pallas_call(
        finish_kernel,
        out_shape=[
            jax.ShapeDtypeStruct((12, 6, 96), F32),
            jax.ShapeDtypeStruct((200, 128), F32),
            jax.ShapeDtypeStruct((80, 200), F32),
        ],
        scratch_shapes=[pltpu.VMEM((200, 128), F32)],
        compiler_params=pltpu.CompilerParams(vmem_limit_bytes=VMEM),
        cost_estimate=pl.CostEstimate(flops=10**8, bytes_accessed=2 << 20, transcendentals=0),
        name="finish",
    )(parts, time_core_t)


def places(move):
    pairs = []
    for source in range(128):
        lon, lat = divmod(source, 16)
        x, y, z, core = (lon % 2) * 2 + lat // 8, lon // 2, lat // 2 % 4, lat % 2
        x, y, z, core = move(x, y, z, core)
        pairs.append((source, (y * 2 + x // 2) * 16 + x % 2 * 8 + z * 2 + core))
    return pairs


OTHER_CORE = places(lambda x, y, z, core: (x, y, z, 1 - core))
Z_STEPS = [places(lambda x, y, z, core: (x, y, (z + step) % 4, core)) for step in range(4)]
X_FLIP = places(lambda x, y, z, core: (x ^ 1, y, z, core))
CHIPS = [[chip // 8 * 16 + chip % 8 * 2 + core for chip in SLOTS] for core in (0, 1)]


def on_device(field, lon_test, lat_test, time_test, lon_core, lat_core, time_core):
    crossed, sums = first_partials(field, lon_core, lon_test.T, lat_test.T, time_test)

    shares = lax.all_to_all(sums, BOTH, 0, 0)
    send, keep = core_partials(crossed, lat_core)
    shares, send, keep = lax.optimization_barrier((shares, send, keep))
    other = lax.ppermute(send, BOTH, OTHER_CORE)
    mine, others = sum_shares(shares)
    others = lax.ppermute(others, BOTH, OTHER_CORE)

    chip = join_shares(keep.reshape(64, 48, 128), other.reshape(64, 48, 128), mine, others)
    parts = lax.all_to_all(chip, BOTH, 0, 0, axis_index_groups=CHIPS)

    field, _ = lax.optimization_barrier((field, chip))
    keep, send = lon_partial(field, lat_test.T, time_test)
    rows = keep + lax.ppermute(send, BOTH, OTHER_CORE)
    total = rows[0]
    for step in range(1, 4):
        total = total + lax.ppermute(rows[step], BOTH, Z_STEPS[step])
    total, parts = lax.optimization_barrier((total, parts))
    sketch_lon = total[0] + lax.ppermute(total[1], BOTH, X_FLIP)

    core_sketch, sketch_lat, sketch_time = finish(parts, time_core.T)
    return (sketch_lon, sketch_lat.T, sketch_time, core_sketch.transpose(2, 0, 1))


def solution(mesh):
    return jax.shard_map(
        on_device,
        mesh=mesh,
        in_specs=(
            P(None, "lon", "lat"),
            P("lon", None),
            P("lat", None),
            P(),
            P(None, "lon"),
            P(None, "lat"),
            P(),
        ),
        out_specs=(P(("lon", "lat"), None), P("lat", None), P(), P(None, "lon", "lat")),
        check_vma=False,
    )
```

```python
import jax
import jax.numpy as jnp
from jax import lax
from jax.experimental import pallas as pl
from jax.experimental.pallas import tpu as pltpu
from jax.sharding import PartitionSpec as P

F32 = jnp.float32
BF16 = jnp.bfloat16
BOTH = ("lon", "lat")
HOURS = 16
VMEM = 48 * 1024 * 1024
MOST_VMEM = 62 * 1024 * 1024
MUCH_VMEM = 40 * 1024 * 1024
SLOTS = sorted(range(64), key=lambda chip: (chip // 16, chip % 4, chip // 8 % 2 * 2 + chip // 4 % 2))


def halves(value):
    top = value.astype(BF16)
    return top, (value - top.astype(F32)).astype(BF16)


def dot(left, right, dims=((1,), (0,))):
    return lax.dot_general(left, right, (dims, ((), ())), preferred_element_type=F32)


def stacked_dot(weights, rows, right_top, right_low):
    upper = dot(weights[...], right_top)
    return upper[:rows] + upper[rows:] + dot(weights[:rows], right_low)


def block_copy(field_hbm, field, arrived, at):
    part = pl.ds(at * HOURS, HOURS)
    return pltpu.make_async_copy(field_hbm.at[part], field.at[part], arrived.at[at])


def start_field(field_hbm, field, arrived, blocks):
    for at in blocks:
        block_copy(field_hbm, field, arrived, at).start()


def each_block(field_hbm, field, arrived, work):
    def step(at, carry):
        block_copy(field_hbm, field, arrived, at).wait()
        work(at)
        return carry

    lax.fori_loop(0, arrived.shape[0], step, 0)


def field_scratch(hours, lons, lats):
    return [pltpu.VMEM((hours, lons, lats), F32), pltpu.SemaphoreType.DMA((hours // HOURS,))]


def copies_in(sources, targets, arrived):
    copies = [pltpu.make_async_copy(a, b, arrived.at[i]) for i, (a, b) in enumerate(zip(sources, targets))]
    for copy in copies:
        copy.start()
    return copies


def in_vmem(count):
    return [pl.BlockSpec(memory_space=pltpu.VMEM)] * count


def in_hbm(count):
    return [pl.BlockSpec(memory_space=pltpu.HBM)] * count


def split_rows(values, weights):
    rows = values.shape[0]
    top, low = halves(values)
    weights[:rows] = top
    weights[rows:] = low


def products(weights, top, low):
    both = stacked_dot(weights, weights.shape[0] // 2, top, low)
    return both[:, :128], both[:, 128:]


def first_kernel(
    field_hbm, modes_hbm, lon_hbm, lat_hbm, time_hbm, crossed_hbm, sums_ref,
    field, arrived, lon_core, lon_test, lat_test, time_test, small, weights, crossed, sent, lat_sum, hour_sum,
):
    modes, rank = lon_core.shape[0], lon_test.shape[0]
    lane = lax.broadcasted_iota(jnp.int32, (rank, 128), 1)
    waits = copies_in((modes_hbm, lon_hbm, lat_hbm, time_hbm), (lon_core, lon_test, lat_test, time_test), small)
    start_field(field_hbm, field, arrived, range(1))
    for total in (lat_sum, hour_sum):
        total[...] = jnp.zeros_like(total)
    for copy in waits:
        copy.wait()
    start_field(field_hbm, field, arrived, range(1, arrived.shape[0]))
    split_rows(jnp.concatenate([lon_core[...], lon_test[...]], axis=0), weights)

    def crossed_copy(at):
        return pltpu.make_async_copy(crossed.at[:, at], crossed_hbm.at[:, at], sent.at[at])

    def work(at):
        times = time_test[pl.ds(at * HOURS, HOURS), :].T
        lat_total, hour_total = lat_sum[...], hour_sum[...]
        for pair in range(0, HOURS, 2):
            first = at * HOURS + pair
            top, low = halves(jnp.concatenate([field[first], field[first + 1]], axis=1))
            for hour, result in enumerate(products(weights, top, low), pair):
                crossed[:, at, hour, :] = result[:modes]
                across = result[modes:]
                lat_total = lat_total + across * times[:, hour : hour + 1]
                total = jnp.sum(across * lat_test[...], axis=1, keepdims=True)
                hour_total = jnp.where(lane == at * HOURS + hour, total, hour_total)
        lat_sum[...] = lat_total
        hour_sum[...] = hour_total
        crossed_copy(at).start()

    each_block(field_hbm, field, arrived, work)
    for place in range(rank // 2):
        columns = slice(place * 2, place * 2 + 2)
        sums_ref[place, 0, :2] = lat_sum[columns]
        sums_ref[place, 0, 2:] = hour_sum[columns]
    sums_ref[rank // 2 :] = jnp.zeros((128 - rank // 2, 1, 4, 128), F32)
    for at in range(arrived.shape[0]):
        crossed_copy(at).wait()


def first_partials(field, lon_core, lon_test_t, lat_test_t, time_test):
    hours, lons, lats = field.shape
    modes, rank = lon_core.shape[0], lon_test_t.shape[0]
    blocks = hours // HOURS
    crossed = (modes, blocks, HOURS, lats)
    return pl.pallas_call(
        first_kernel,
        in_specs=in_hbm(5),
        out_specs=[pl.BlockSpec(memory_space=pl.ANY)] + in_vmem(1),
        out_shape=[jax.ShapeDtypeStruct(crossed, F32), jax.ShapeDtypeStruct((128, 1, 4, 128), F32)],
        scratch_shapes=field_scratch(hours, lons, lats)
        + [pltpu.VMEM(x.shape, F32) for x in (lon_core, lon_test_t, lat_test_t, time_test)]
        + [
            pltpu.SemaphoreType.DMA((4,)),
            pltpu.VMEM((2 * (modes + rank), lons), BF16),
            pltpu.VMEM(crossed, F32),
            pltpu.SemaphoreType.DMA((blocks,)),
            pltpu.VMEM((rank, 128), F32),
            pltpu.VMEM((rank, 128), F32),
        ],
        compiler_params=pltpu.CompilerParams(vmem_limit_bytes=MOST_VMEM),
        cost_estimate=pl.CostEstimate(flops=18 * 10**9, bytes_accessed=26 << 20, transcendentals=0),
        name="first_partials",
    )(field, lon_core, lon_test_t, lat_test_t, time_test)


def sum_kernel(shares_ref, keep_ref, send_ref):
    core = lax.axis_index("lat") % 2
    mine = lax.broadcasted_iota(jnp.int32, (4, 128), 0) // 2 == core

    def spread(rows):
        return jnp.where(mine, jnp.concatenate([rows, rows], axis=0), 0.0)

    hour = jnp.zeros((4, 128), F32)
    for at in range(8):
        lats = []
        for lat in (at * 2, at * 2 + 1):
            total = shares_ref[lat, 0]
            for lon in range(1, 8):
                total = total + shares_ref[lon * 16 + lat, 0]
            hour = hour + total
            lats.append(spread(total[:2]))
        tile, row = at // 2, at % 2 * 4
        keep_ref[tile, row : row + 4] = jnp.where(core == 0, lats[0], lats[1])
        send_ref[tile, row : row + 4] = jnp.where(core == 0, lats[1], lats[0])
    hour = spread(hour[2:])
    for out in (keep_ref, send_ref):
        out[4, :4] = hour
        out[4, 4:] = hour


def sum_shares(shares):
    return pl.pallas_call(
        sum_kernel,
        out_shape=[jax.ShapeDtypeStruct((5, 8, 128), F32)] * 2,
        compiler_params=pltpu.CompilerParams(vmem_limit_bytes=MUCH_VMEM),
        cost_estimate=pl.CostEstimate(flops=10**6, bytes_accessed=1 << 20, transcendentals=0),
        name="sum_shares",
    )(shares)


def core_kernel(crossed, lat_ref, send_ref, keep_ref, lat_core):
    lat_core[:96] = lat_ref[...]
    lat_core[96:] = jnp.zeros((16, 128), F32)

    core = lax.axis_index("lat") % 2
    of_core = [
        jnp.concatenate([lat_core[pl.ds(at * 6 + b, 8, stride=12), :] for b in range(6)], axis=0) for at in range(2)
    ]
    lat_rows = jnp.concatenate(
        [jnp.where(core == 0, of_core[0], of_core[1]), jnp.where(core == 0, of_core[1], of_core[0])], axis=0
    )
    lat_top, lat_low = halves(lat_rows)
    lats = jnp.concatenate(
        [jnp.concatenate([lat_top, lat_top], axis=1), jnp.concatenate([lat_low, jnp.zeros_like(lat_low)], axis=1)],
        axis=0,
    )

    def share(owner, carry):
        block = crossed[pl.ds(owner * 12, 12)].reshape(960, 128)
        block = jnp.concatenate([block, jnp.zeros((64, 128), F32)], axis=0)
        result = dot(lats, jnp.concatenate(halves(block), axis=1), ((1,), (1,)))
        result = result[:96] + result[96:]
        for part, out in enumerate((keep_ref, send_ref)):
            for b in range(6):
                row = part * 48 + b * 8
                for q in range(8):
                    out[owner, :, q * 6 + b, :] = result[row : row + 8, q * 128 : q * 128 + 128]
        return carry

    lax.fori_loop(0, 8, share, 0)


def core_partials(crossed, lat_core):
    part = jax.ShapeDtypeStruct((8, 8, 48, 128), F32)
    return pl.pallas_call(
        core_kernel,
        in_specs=in_vmem(2),
        out_specs=in_vmem(2),
        out_shape=[part, part],
        scratch_shapes=[pltpu.VMEM((112, 128), F32)],
        compiler_params=pltpu.CompilerParams(vmem_limit_bytes=MUCH_VMEM),
        cost_estimate=pl.CostEstimate(flops=20 * 10**9, bytes_accessed=8 << 20, transcendentals=0),
        name="core_partials",
    )(crossed, lat_core)


def join_kernel(keep_ref, arrived_ref, mine_ref, other_ref, out_ref, sums):
    sums[...] = mine_ref[...] + other_ref[...]
    for slot, chip in enumerate(SLOTS):
        lat = chip % 8
        row = lat % 2 * 4
        out_ref[slot, :48] = keep_ref[chip] + arrived_ref[chip]
        out_ref[slot, 48:52] = sums[lat // 2, row : row + 4]
        out_ref[slot, 52:] = sums[4, :4]


def join_shares(keep, arrived, mine, other):
    return pl.pallas_call(
        join_kernel,
        in_specs=in_vmem(4),
        out_specs=pl.BlockSpec(memory_space=pltpu.VMEM),
        out_shape=jax.ShapeDtypeStruct((64, 56, 128), F32),
        scratch_shapes=[pltpu.VMEM(mine.shape, F32)],
        compiler_params=pltpu.CompilerParams(vmem_limit_bytes=MUCH_VMEM),
        cost_estimate=pl.CostEstimate(flops=10**6, bytes_accessed=5 << 20, transcendentals=0),
        name="join_shares",
    )(keep, arrived, mine, other)


def lon_kernel(field_hbm, lat_ref, time_ref, keep_ref, send_ref, field, arrived, lat_test, total):
    start_field(field_hbm, field, arrived, range(arrived.shape[0]))
    total[...] = jnp.zeros_like(total)
    lat_test[...] = lat_ref[...].T
    lons = total.shape[0]

    def work(at):
        times = time_ref[pl.ds(at * HOURS, HOURS), :]
        tests = [lat_test[...] * times[hour : hour + 1, :] for hour in range(HOURS)]
        test_top, test_low = halves(jnp.concatenate(tests, axis=0))
        values = [halves(field[at * HOURS + hour]) for hour in range(HOURS)]
        top = jnp.concatenate([value[0] for value in values], axis=1)
        low = jnp.concatenate([value[1] for value in values], axis=1)
        upper = dot(jnp.concatenate([top, low], axis=0), test_top)
        total[...] += upper[:lons] + upper[lons:] + dot(top, test_low)

    each_block(field_hbm, field, arrived, work)
    place = lax.axis_index("lat")
    core, z, x_lo = place % 2, place // 2 % 4, place // 8
    for step in range(4):
        for flip in range(2):
            x = x_lo + flip - 2 * x_lo * flip
            owner = x * 8 + (z + step) % 4 * 2
            for out, of_core in ((keep_ref, core), (send_ref, 1 - core)):
                out[step, flip] = total[pl.ds(pl.multiple_of((owner + of_core) * 32, 32), 32), :]


def lon_partial(field, lat_test_t, time_test):
    hours, lons, lats = field.shape
    rank = lat_test_t.shape[0]
    out = jax.ShapeDtypeStruct((4, 2, 32, rank), F32)
    return pl.pallas_call(
        lon_kernel,
        in_specs=in_hbm(1) + in_vmem(2),
        out_specs=in_vmem(2),
        out_shape=[out, out],
        scratch_shapes=field_scratch(hours, lons, lats)
        + [pltpu.VMEM((lats, rank), F32), pltpu.VMEM((lons, rank), F32)],
        compiler_params=pltpu.CompilerParams(vmem_limit_bytes=MUCH_VMEM),
        cost_estimate=pl.CostEstimate(flops=12 * 10**9, bytes_accessed=22 << 20, transcendentals=0),
        name="lon_partial",
    )(field, lat_test_t, time_test)


def finish_kernel(parts_ref, time_ref, core_ref, lat_ref, hour_ref, columns):
    total = parts_ref[0, :48]
    for source in range(1, parts_ref.shape[0]):
        total = total + parts_ref[source, :48]
    modes = [jnp.concatenate([total[q * 6 : q * 6 + 6], jnp.zeros((2, 128), F32)], axis=0) for q in range(8)]
    modes = jnp.concatenate(modes, axis=1)
    rows = jnp.concatenate([modes[:, a * 80 : a * 80 + 80] for a in range(12)], axis=0)
    result = lax.dot_general(
        rows,
        time_ref[...],
        (((1,), (0,)), ((), ())),
        precision=lax.Precision.HIGHEST,
        preferred_element_type=F32,
    )
    for a in range(12):
        core_ref[a] = result[a * 8 : a * 8 + 6]
    for slot, chip in enumerate(SLOTS):
        if chip < 50:
            lat_ref[chip * 4 : chip * 4 + 4] = parts_ref[slot, 48:52]
            columns[chip * 4 : chip * 4 + 4] = parts_ref[slot, 52:]
    hour_ref[...] = columns[...].T[:80]


def finish(parts, time_core_t):
    return pl.pallas_call(
        finish_kernel,
        out_shape=[
            jax.ShapeDtypeStruct((12, 6, 96), F32),
            jax.ShapeDtypeStruct((200, 128), F32),
            jax.ShapeDtypeStruct((80, 200), F32),
        ],
        scratch_shapes=[pltpu.VMEM((200, 128), F32)],
        compiler_params=pltpu.CompilerParams(vmem_limit_bytes=VMEM),
        cost_estimate=pl.CostEstimate(flops=10**8, bytes_accessed=2 << 20, transcendentals=0),
        name="finish",
    )(parts, time_core_t)


def places(move):
    pairs = []
    for source in range(128):
        lon, lat = divmod(source, 16)
        x, y, z, core = (lon % 2) * 2 + lat // 8, lon // 2, lat // 2 % 4, lat % 2
        x, y, z, core = move(x, y, z, core)
        pairs.append((source, (y * 2 + x // 2) * 16 + x % 2 * 8 + z * 2 + core))
    return pairs


OTHER_CORE = places(lambda x, y, z, core: (x, y, z, 1 - core))
Z_STEPS = [places(lambda x, y, z, core: (x, y, (z + step) % 4, core)) for step in range(4)]
X_FLIP = places(lambda x, y, z, core: (x ^ 1, y, z, core))
CHIPS = [[chip // 8 * 16 + chip % 8 * 2 + core for chip in SLOTS] for core in (0, 1)]


def on_device(field, lon_test, lat_test, time_test, lon_core, lat_core, time_core):
    crossed, sums = first_partials(field, lon_core, lon_test.T, lat_test.T, time_test)

    shares = lax.all_to_all(sums, BOTH, 0, 0)
    send, keep = core_partials(crossed, lat_core)
    shares, send, keep = lax.optimization_barrier((shares, send, keep))
    other = lax.ppermute(send, BOTH, OTHER_CORE)
    mine, others = sum_shares(shares)
    others = lax.ppermute(others, BOTH, OTHER_CORE)

    chip = join_shares(keep.reshape(64, 48, 128), other.reshape(64, 48, 128), mine, others)
    parts = lax.all_to_all(chip, BOTH, 0, 0, axis_index_groups=CHIPS)

    field, _ = lax.optimization_barrier((field, chip))
    keep, send = lon_partial(field, lat_test.T, time_test)
    rows = keep + lax.ppermute(send, BOTH, OTHER_CORE)
    total = rows[0]
    for step in range(1, 4):
        total = total + lax.ppermute(rows[step], BOTH, Z_STEPS[step])
    total, parts = lax.optimization_barrier((total, parts))
    sketch_lon = total[0] + lax.ppermute(total[1], BOTH, X_FLIP)

    core_sketch, sketch_lat, sketch_time = finish(parts, time_core.T)
    return (sketch_lon, sketch_lat.T, sketch_time, core_sketch.transpose(2, 0, 1))


def solution(mesh):
    return jax.shard_map(
        on_device,
        mesh=mesh,
        in_specs=(
            P(None, "lon", "lat"),
            P("lon", None),
            P("lat", None),
            P(),
            P(None, "lon"),
            P(None, "lat"),
            P(),
        ),
        out_specs=(P(("lon", "lat"), None), P("lat", None), P(), P(None, "lon", "lat")),
        check_vma=False,
    )
```

```python
import jax
import jax.numpy as jnp
from jax import lax
from jax.experimental import pallas as pl
from jax.experimental.pallas import tpu as pltpu
from jax.sharding import PartitionSpec as P

F32 = jnp.float32
BF16 = jnp.bfloat16
BOTH = ("lon", "lat")
HOURS = 16
VMEM = 48 * 1024 * 1024
MOST_VMEM = 62 * 1024 * 1024
MUCH_VMEM = 40 * 1024 * 1024
MORE_VMEM = 50 * 1024 * 1024
SLOTS = sorted(range(64), key=lambda chip: (chip // 16, chip % 4, chip // 8 % 2 * 2 + chip // 4 % 2))


def halves(value):
    top = value.astype(BF16)
    return top, (value - top.astype(F32)).astype(BF16)


def dot(left, right, dims=((1,), (0,))):
    return lax.dot_general(left, right, (dims, ((), ())), preferred_element_type=F32)


def stacked_dot(weights, rows, right_top, right_low):
    upper = dot(weights[...], right_top)
    return upper[:rows] + upper[rows:] + dot(weights[:rows], right_low)


def block_copy(field_hbm, field, arrived, at):
    part = pl.ds(at * HOURS, HOURS)
    return pltpu.make_async_copy(field_hbm.at[part], field.at[part], arrived.at[at])


def start_field(field_hbm, field, arrived, blocks):
    for at in blocks:
        block_copy(field_hbm, field, arrived, at).start()


def each_block(field_hbm, field, arrived, work):
    def step(at, carry):
        block_copy(field_hbm, field, arrived, at).wait()
        work(at)
        return carry

    lax.fori_loop(0, arrived.shape[0], step, 0)


def field_scratch(hours, lons, lats):
    return [pltpu.VMEM((hours, lons, lats), F32), pltpu.SemaphoreType.DMA((hours // HOURS,))]


def copies_in(sources, targets, arrived):
    copies = [pltpu.make_async_copy(a, b, arrived.at[i]) for i, (a, b) in enumerate(zip(sources, targets))]
    for copy in copies:
        copy.start()
    return copies


def in_vmem(count):
    return [pl.BlockSpec(memory_space=pltpu.VMEM)] * count


def in_hbm(count):
    return [pl.BlockSpec(memory_space=pltpu.HBM)] * count


def split_rows(values, weights):
    rows = values.shape[0]
    top, low = halves(values)
    weights[:rows] = top
    weights[rows:] = low


def products(weights, top, low):
    both = stacked_dot(weights, weights.shape[0] // 2, top, low)
    return both[:, :128], both[:, 128:]


def first_kernel(
    field_hbm, modes_hbm, lon_hbm, lat_hbm, time_hbm, crossed_hbm, sums_ref,
    field, arrived, lon_core, lon_test, lat_test, time_test, small, weights, crossed, sent, lat_sum, hour_sum,
):
    modes, rank = lon_core.shape[0], lon_test.shape[0]
    lane = lax.broadcasted_iota(jnp.int32, (rank, 128), 1)
    waits = copies_in((modes_hbm, lon_hbm, lat_hbm, time_hbm), (lon_core, lon_test, lat_test, time_test), small)
    start_field(field_hbm, field, arrived, range(1))
    for total in (lat_sum, hour_sum):
        total[...] = jnp.zeros_like(total)
    for copy in waits:
        copy.wait()
    start_field(field_hbm, field, arrived, range(1, arrived.shape[0]))
    split_rows(jnp.concatenate([lon_core[...], lon_test[...]], axis=0), weights)

    def crossed_copy(at):
        return pltpu.make_async_copy(crossed.at[:, at], crossed_hbm.at[:, at], sent.at[at])

    def work(at):
        times = time_test[pl.ds(at * HOURS, HOURS), :].T
        lat_total, hour_total = lat_sum[...], hour_sum[...]
        for pair in range(0, HOURS, 2):
            first = at * HOURS + pair
            top, low = halves(jnp.concatenate([field[first], field[first + 1]], axis=1))
            for hour, result in enumerate(products(weights, top, low), pair):
                crossed[:, at, hour, :] = result[:modes]
                across = result[modes:]
                lat_total = lat_total + across * times[:, hour : hour + 1]
                total = jnp.sum(across * lat_test[...], axis=1, keepdims=True)
                hour_total = jnp.where(lane == at * HOURS + hour, total, hour_total)
        lat_sum[...] = lat_total
        hour_sum[...] = hour_total
        crossed_copy(at).start()

    each_block(field_hbm, field, arrived, work)
    for place in range(rank // 2):
        columns = slice(place * 2, place * 2 + 2)
        sums_ref[place, 0, :2] = lat_sum[columns]
        sums_ref[place, 0, 2:] = hour_sum[columns]
    sums_ref[rank // 2 :] = jnp.zeros((128 - rank // 2, 1, 4, 128), F32)
    for at in range(arrived.shape[0]):
        crossed_copy(at).wait()


def first_partials(field, lon_core, lon_test_t, lat_test_t, time_test):
    hours, lons, lats = field.shape
    modes, rank = lon_core.shape[0], lon_test_t.shape[0]
    blocks = hours // HOURS
    crossed = (modes, blocks, HOURS, lats)
    return pl.pallas_call(
        first_kernel,
        in_specs=in_hbm(5),
        out_specs=[pl.BlockSpec(memory_space=pl.ANY)] + in_vmem(1),
        out_shape=[jax.ShapeDtypeStruct(crossed, F32), jax.ShapeDtypeStruct((128, 1, 4, 128), F32)],
        scratch_shapes=field_scratch(hours, lons, lats)
        + [pltpu.VMEM(x.shape, F32) for x in (lon_core, lon_test_t, lat_test_t, time_test)]
        + [
            pltpu.SemaphoreType.DMA((4,)),
            pltpu.VMEM((2 * (modes + rank), lons), BF16),
            pltpu.VMEM(crossed, F32),
            pltpu.SemaphoreType.DMA((blocks,)),
            pltpu.VMEM((rank, 128), F32),
            pltpu.VMEM((rank, 128), F32),
        ],
        compiler_params=pltpu.CompilerParams(vmem_limit_bytes=MOST_VMEM),
        cost_estimate=pl.CostEstimate(flops=18 * 10**9, bytes_accessed=26 << 20, transcendentals=0),
        name="first_partials",
    )(field, lon_core, lon_test_t, lat_test_t, time_test)


def sum_kernel(shares_ref, keep_ref, send_ref):
    core = lax.axis_index("lat") % 2
    mine = lax.broadcasted_iota(jnp.int32, (4, 128), 0) // 2 == core

    def spread(rows):
        return jnp.where(mine, jnp.concatenate([rows, rows], axis=0), 0.0)

    hour = jnp.zeros((4, 128), F32)
    for at in range(8):
        lats = []
        for lat in (at * 2, at * 2 + 1):
            total = shares_ref[lat, 0]
            for lon in range(1, 8):
                total = total + shares_ref[lon * 16 + lat, 0]
            hour = hour + total
            lats.append(spread(total[:2]))
        tile, row = at // 2, at % 2 * 4
        keep_ref[tile, row : row + 4] = jnp.where(core == 0, lats[0], lats[1])
        send_ref[tile, row : row + 4] = jnp.where(core == 0, lats[1], lats[0])
    hour = spread(hour[2:])
    for out in (keep_ref, send_ref):
        out[4, :4] = hour
        out[4, 4:] = hour


def sum_shares(shares):
    return pl.pallas_call(
        sum_kernel,
        out_shape=[jax.ShapeDtypeStruct((5, 8, 128), F32)] * 2,
        compiler_params=pltpu.CompilerParams(vmem_limit_bytes=MUCH_VMEM),
        cost_estimate=pl.CostEstimate(flops=10**6, bytes_accessed=1 << 20, transcendentals=0),
        name="sum_shares",
    )(shares)


def core_kernel(crossed_hbm, lat_ref, send_ref, keep_ref, lat_core, crossed, arrived):
    def crossed_copy(owner):
        part = pl.ds(owner * 12, 12)
        return pltpu.make_async_copy(crossed_hbm.at[part], crossed.at[part], arrived.at[owner])

    for owner in range(8):
        crossed_copy(owner).start()
    lat_core[:96] = lat_ref[...]
    lat_core[96:] = jnp.zeros((16, 128), F32)

    core = lax.axis_index("lat") % 2
    of_core = [
        jnp.concatenate([lat_core[pl.ds(at * 6 + b, 8, stride=12), :] for b in range(6)], axis=0) for at in range(2)
    ]
    lat_rows = jnp.concatenate(
        [jnp.where(core == 0, of_core[0], of_core[1]), jnp.where(core == 0, of_core[1], of_core[0])], axis=0
    )
    lat_top, lat_low = halves(lat_rows)
    lats = jnp.concatenate(
        [jnp.concatenate([lat_top, lat_top], axis=1), jnp.concatenate([lat_low, jnp.zeros_like(lat_low)], axis=1)],
        axis=0,
    )

    def share(owner, carry):
        crossed_copy(owner).wait()
        block = crossed[pl.ds(owner * 12, 12)].reshape(960, 128)
        block = jnp.concatenate([block, jnp.zeros((64, 128), F32)], axis=0)
        result = dot(lats, jnp.concatenate(halves(block), axis=1), ((1,), (1,)))
        result = result[:96] + result[96:]
        for part, out in enumerate((keep_ref, send_ref)):
            for b in range(6):
                row = part * 48 + b * 8
                for q in range(8):
                    out[owner, :, q * 6 + b, :] = result[row : row + 8, q * 128 : q * 128 + 128]
        return carry

    lax.fori_loop(0, 8, share, 0)


def core_partials(crossed, lat_core):
    part = jax.ShapeDtypeStruct((8, 8, 48, 128), F32)
    return pl.pallas_call(
        core_kernel,
        in_specs=[pl.BlockSpec(memory_space=pl.ANY)] + in_vmem(1),
        out_specs=in_vmem(2),
        out_shape=[part, part],
        scratch_shapes=[
            pltpu.VMEM((112, 128), F32),
            pltpu.VMEM(crossed.shape, F32),
            pltpu.SemaphoreType.DMA((8,)),
        ],
        compiler_params=pltpu.CompilerParams(vmem_limit_bytes=MORE_VMEM),
        cost_estimate=pl.CostEstimate(flops=20 * 10**9, bytes_accessed=8 << 20, transcendentals=0),
        name="core_partials",
    )(crossed, lat_core)


def join_kernel(keep_ref, arrived_ref, mine_ref, other_ref, out_hbm, out, sums, sent):
    sums[...] = mine_ref[...] + other_ref[...]
    copies = []
    for slot, chip in enumerate(SLOTS):
        lat = chip % 8
        row = lat % 2 * 4
        out[slot, :48] = keep_ref[chip] + arrived_ref[chip]
        out[slot, 48:52] = sums[lat // 2, row : row + 4]
        out[slot, 52:] = sums[4, :4]
        if slot % 8 == 7:
            piece = pl.ds(slot - 7, 8)
            copies.append(pltpu.make_async_copy(out.at[piece], out_hbm.at[piece], sent.at[slot // 8]))
            copies[-1].start()
    for copy in copies:
        copy.wait()


def join_shares(keep, arrived, mine, other):
    shape = (64, 56, 128)
    return pl.pallas_call(
        join_kernel,
        in_specs=in_vmem(4),
        out_specs=pl.BlockSpec(memory_space=pl.ANY),
        out_shape=jax.ShapeDtypeStruct(shape, F32),
        scratch_shapes=[pltpu.VMEM(shape, F32), pltpu.VMEM(mine.shape, F32), pltpu.SemaphoreType.DMA((8,))],
        compiler_params=pltpu.CompilerParams(vmem_limit_bytes=MORE_VMEM),
        cost_estimate=pl.CostEstimate(flops=10**6, bytes_accessed=5 << 20, transcendentals=0),
        name="join_shares",
    )(keep, arrived, mine, other)


def lon_kernel(field_hbm, lat_ref, time_ref, keep_ref, send_ref, field, arrived, lat_test, total):
    start_field(field_hbm, field, arrived, range(arrived.shape[0]))
    total[...] = jnp.zeros_like(total)
    lat_test[...] = lat_ref[...].T
    lons = total.shape[0]

    def work(at):
        times = time_ref[pl.ds(at * HOURS, HOURS), :]
        tests = [lat_test[...] * times[hour : hour + 1, :] for hour in range(HOURS)]
        test_top, test_low = halves(jnp.concatenate(tests, axis=0))
        values = [halves(field[at * HOURS + hour]) for hour in range(HOURS)]
        top = jnp.concatenate([value[0] for value in values], axis=1)
        low = jnp.concatenate([value[1] for value in values], axis=1)
        upper = dot(jnp.concatenate([top, low], axis=0), test_top)
        total[...] += upper[:lons] + upper[lons:] + dot(top, test_low)

    each_block(field_hbm, field, arrived, work)
    place = lax.axis_index("lat")
    core, z, x_lo = place % 2, place // 2 % 4, place // 8
    for step in range(4):
        for flip in range(2):
            x = x_lo + flip - 2 * x_lo * flip
            owner = x * 8 + (z + step) % 4 * 2
            for out, of_core in ((keep_ref, core), (send_ref, 1 - core)):
                out[step, flip] = total[pl.ds(pl.multiple_of((owner + of_core) * 32, 32), 32), :]


def lon_partial(field, lat_test_t, time_test):
    hours, lons, lats = field.shape
    rank = lat_test_t.shape[0]
    out = jax.ShapeDtypeStruct((4, 2, 32, rank), F32)
    return pl.pallas_call(
        lon_kernel,
        in_specs=in_hbm(1) + in_vmem(2),
        out_specs=in_vmem(2),
        out_shape=[out, out],
        scratch_shapes=field_scratch(hours, lons, lats)
        + [pltpu.VMEM((lats, rank), F32), pltpu.VMEM((lons, rank), F32)],
        compiler_params=pltpu.CompilerParams(vmem_limit_bytes=MUCH_VMEM),
        cost_estimate=pl.CostEstimate(flops=12 * 10**9, bytes_accessed=22 << 20, transcendentals=0),
        name="lon_partial",
    )(field, lat_test_t, time_test)


def finish_kernel(parts_ref, time_ref, core_ref, lat_ref, hour_ref, columns):
    total = parts_ref[0, :48]
    for source in range(1, parts_ref.shape[0]):
        total = total + parts_ref[source, :48]
    modes = [jnp.concatenate([total[q * 6 : q * 6 + 6], jnp.zeros((2, 128), F32)], axis=0) for q in range(8)]
    modes = jnp.concatenate(modes, axis=1)
    rows = jnp.concatenate([modes[:, a * 80 : a * 80 + 80] for a in range(12)], axis=0)
    result = lax.dot_general(
        rows,
        time_ref[...],
        (((1,), (0,)), ((), ())),
        precision=lax.Precision.HIGHEST,
        preferred_element_type=F32,
    )
    for a in range(12):
        core_ref[a] = result[a * 8 : a * 8 + 6]
    for slot, chip in enumerate(SLOTS):
        if chip < 50:
            lat_ref[chip * 4 : chip * 4 + 4] = parts_ref[slot, 48:52]
            columns[chip * 4 : chip * 4 + 4] = parts_ref[slot, 52:]
    hour_ref[...] = columns[...].T[:80]


def finish(parts, time_core_t):
    return pl.pallas_call(
        finish_kernel,
        out_shape=[
            jax.ShapeDtypeStruct((12, 6, 96), F32),
            jax.ShapeDtypeStruct((200, 128), F32),
            jax.ShapeDtypeStruct((80, 200), F32),
        ],
        scratch_shapes=[pltpu.VMEM((200, 128), F32)],
        compiler_params=pltpu.CompilerParams(vmem_limit_bytes=VMEM),
        cost_estimate=pl.CostEstimate(flops=10**8, bytes_accessed=2 << 20, transcendentals=0),
        name="finish",
    )(parts, time_core_t)


def places(move):
    pairs = []
    for source in range(128):
        lon, lat = divmod(source, 16)
        x, y, z, core = (lon % 2) * 2 + lat // 8, lon // 2, lat // 2 % 4, lat % 2
        x, y, z, core = move(x, y, z, core)
        pairs.append((source, (y * 2 + x // 2) * 16 + x % 2 * 8 + z * 2 + core))
    return pairs


OTHER_CORE = places(lambda x, y, z, core: (x, y, z, 1 - core))
Z_STEPS = [places(lambda x, y, z, core: (x, y, (z + step) % 4, core)) for step in range(4)]
X_FLIP = places(lambda x, y, z, core: (x ^ 1, y, z, core))
CHIPS = [[chip // 8 * 16 + chip % 8 * 2 + core for chip in SLOTS] for core in (0, 1)]


def on_device(field, lon_test, lat_test, time_test, lon_core, lat_core, time_core):
    crossed, sums = first_partials(field, lon_core, lon_test.T, lat_test.T, time_test)

    shares = lax.all_to_all(sums, BOTH, 0, 0)
    send, keep = core_partials(crossed, lat_core)
    shares, send, keep = lax.optimization_barrier((shares, send, keep))
    other = lax.ppermute(send, BOTH, OTHER_CORE)
    mine, others = sum_shares(shares)
    others = lax.ppermute(others, BOTH, OTHER_CORE)

    chip = join_shares(keep.reshape(64, 48, 128), other.reshape(64, 48, 128), mine, others)
    parts = lax.all_to_all(chip, BOTH, 0, 0, axis_index_groups=CHIPS)

    field, _ = lax.optimization_barrier((field, chip))
    keep, send = lon_partial(field, lat_test.T, time_test)
    rows = keep + lax.ppermute(send, BOTH, OTHER_CORE)
    total = rows[0]
    for step in range(1, 4):
        total = total + lax.ppermute(rows[step], BOTH, Z_STEPS[step])
    total, parts = lax.optimization_barrier((total, parts))
    sketch_lon = total[0] + lax.ppermute(total[1], BOTH, X_FLIP)

    core_sketch, sketch_lat, sketch_time = finish(parts, time_core.T)
    return (sketch_lon, sketch_lat.T, sketch_time, core_sketch.transpose(2, 0, 1))


def solution(mesh):
    return jax.shard_map(
        on_device,
        mesh=mesh,
        in_specs=(
            P(None, "lon", "lat"),
            P("lon", None),
            P("lat", None),
            P(),
            P(None, "lon"),
            P(None, "lat"),
            P(),
        ),
        out_specs=(P(("lon", "lat"), None), P("lat", None), P(), P(None, "lon", "lat")),
        check_vma=False,
    )
```

```python
import jax
import jax.numpy as jnp
from jax import lax
from jax.experimental import pallas as pl
from jax.experimental.pallas import tpu as pltpu
from jax.sharding import PartitionSpec as P

F32 = jnp.float32
BF16 = jnp.bfloat16
BOTH = ("lon", "lat")
HOURS = 16
VMEM = 48 * 1024 * 1024
MOST_VMEM = 62 * 1024 * 1024
MUCH_VMEM = 40 * 1024 * 1024
MORE_VMEM = 50 * 1024 * 1024
SLOTS = sorted(range(64), key=lambda chip: (chip // 16, chip % 4, chip // 8 % 2 * 2 + chip // 4 % 2))


def halves(value):
    top = value.astype(BF16)
    return top, (value - top.astype(F32)).astype(BF16)


def dot(left, right, dims=((1,), (0,))):
    return lax.dot_general(left, right, (dims, ((), ())), preferred_element_type=F32)


def stacked_dot(weights, rows, right_top, right_low):
    upper = dot(weights[...], right_top)
    return upper[:rows] + upper[rows:] + dot(weights[:rows], right_low)


def block_copy(field_hbm, field, arrived, at):
    part = pl.ds(at * HOURS, HOURS)
    return pltpu.make_async_copy(field_hbm.at[part], field.at[part], arrived.at[at])


def start_field(field_hbm, field, arrived, blocks):
    for at in blocks:
        block_copy(field_hbm, field, arrived, at).start()


def each_block(field_hbm, field, arrived, work):
    def step(at, carry):
        block_copy(field_hbm, field, arrived, at).wait()

        @pl.when(at + 2 < arrived.shape[0])
        def _():
            block_copy(field_hbm, field, arrived, at + 2).start()

        work(at)
        return carry

    lax.fori_loop(0, arrived.shape[0], step, 0)


def field_scratch(hours, lons, lats):
    return [pltpu.VMEM((hours, lons, lats), F32), pltpu.SemaphoreType.DMA((hours // HOURS,))]


def copies_in(sources, targets, arrived):
    copies = [pltpu.make_async_copy(a, b, arrived.at[i]) for i, (a, b) in enumerate(zip(sources, targets))]
    for copy in copies:
        copy.start()
    return copies


def in_vmem(count):
    return [pl.BlockSpec(memory_space=pltpu.VMEM)] * count


def in_hbm(count):
    return [pl.BlockSpec(memory_space=pltpu.HBM)] * count


def split_rows(values, weights):
    rows = values.shape[0]
    top, low = halves(values)
    weights[:rows] = top
    weights[rows:] = low


def products(weights, top, low):
    both = stacked_dot(weights, weights.shape[0] // 2, top, low)
    return both[:, :128], both[:, 128:]


def first_kernel(
    field_hbm, modes_hbm, lon_hbm, lat_hbm, time_hbm, crossed_hbm, sums_ref,
    field, arrived, lon_core, lon_test, lat_test, time_test, small, weights, crossed, sent, lat_sum, hour_sum,
):
    modes, rank = lon_core.shape[0], lon_test.shape[0]
    lane = lax.broadcasted_iota(jnp.int32, (rank, 128), 1)
    waits = copies_in((modes_hbm, lon_hbm, lat_hbm, time_hbm), (lon_core, lon_test, lat_test, time_test), small)
    start_field(field_hbm, field, arrived, range(1))
    for total in (lat_sum, hour_sum):
        total[...] = jnp.zeros_like(total)
    for copy in waits:
        copy.wait()
    start_field(field_hbm, field, arrived, range(1, 2))
    split_rows(jnp.concatenate([lon_core[...], lon_test[...]], axis=0), weights)

    def crossed_copy(at):
        return pltpu.make_async_copy(crossed.at[:, at], crossed_hbm.at[:, at], sent.at[at])

    def work(at):
        times = time_test[pl.ds(at * HOURS, HOURS), :].T
        lat_total, hour_total = lat_sum[...], hour_sum[...]
        for pair in range(0, HOURS, 2):
            first = at * HOURS + pair
            top, low = halves(jnp.concatenate([field[first], field[first + 1]], axis=1))
            for hour, result in enumerate(products(weights, top, low), pair):
                crossed[:, at, hour, :] = result[:modes]
                across = result[modes:]
                lat_total = lat_total + across * times[:, hour : hour + 1]
                total = jnp.sum(across * lat_test[...], axis=1, keepdims=True)
                hour_total = jnp.where(lane == at * HOURS + hour, total, hour_total)
        lat_sum[...] = lat_total
        hour_sum[...] = hour_total
        crossed_copy(at).start()

    each_block(field_hbm, field, arrived, work)
    for place in range(rank // 2):
        columns = slice(place * 2, place * 2 + 2)
        sums_ref[place, 0, :2] = lat_sum[columns]
        sums_ref[place, 0, 2:] = hour_sum[columns]
    sums_ref[rank // 2 :] = jnp.zeros((128 - rank // 2, 1, 4, 128), F32)
    for at in range(arrived.shape[0]):
        crossed_copy(at).wait()


def first_partials(field, lon_core, lon_test_t, lat_test_t, time_test):
    hours, lons, lats = field.shape
    modes, rank = lon_core.shape[0], lon_test_t.shape[0]
    blocks = hours // HOURS
    crossed = (modes, blocks, HOURS, lats)
    return pl.pallas_call(
        first_kernel,
        in_specs=in_hbm(5),
        out_specs=[pl.BlockSpec(memory_space=pl.ANY)] + in_vmem(1),
        out_shape=[jax.ShapeDtypeStruct(crossed, F32), jax.ShapeDtypeStruct((128, 1, 4, 128), F32)],
        scratch_shapes=field_scratch(hours, lons, lats)
        + [pltpu.VMEM(x.shape, F32) for x in (lon_core, lon_test_t, lat_test_t, time_test)]
        + [
            pltpu.SemaphoreType.DMA((4,)),
            pltpu.VMEM((2 * (modes + rank), lons), BF16),
            pltpu.VMEM(crossed, F32),
            pltpu.SemaphoreType.DMA((blocks,)),
            pltpu.VMEM((rank, 128), F32),
            pltpu.VMEM((rank, 128), F32),
        ],
        compiler_params=pltpu.CompilerParams(vmem_limit_bytes=MOST_VMEM),
        cost_estimate=pl.CostEstimate(flops=18 * 10**9, bytes_accessed=26 << 20, transcendentals=0),
        name="first_partials",
    )(field, lon_core, lon_test_t, lat_test_t, time_test)


def sum_kernel(shares_ref, keep_ref, send_ref):
    core = lax.axis_index("lat") % 2
    mine = lax.broadcasted_iota(jnp.int32, (4, 128), 0) // 2 == core

    def spread(rows):
        return jnp.where(mine, jnp.concatenate([rows, rows], axis=0), 0.0)

    hour = jnp.zeros((4, 128), F32)
    for at in range(8):
        lats = []
        for lat in (at * 2, at * 2 + 1):
            total = shares_ref[lat, 0]
            for lon in range(1, 8):
                total = total + shares_ref[lon * 16 + lat, 0]
            hour = hour + total
            lats.append(spread(total[:2]))
        tile, row = at // 2, at % 2 * 4
        keep_ref[tile, row : row + 4] = jnp.where(core == 0, lats[0], lats[1])
        send_ref[tile, row : row + 4] = jnp.where(core == 0, lats[1], lats[0])
    hour = spread(hour[2:])
    for out in (keep_ref, send_ref):
        out[4, :4] = hour
        out[4, 4:] = hour


def sum_shares(shares):
    return pl.pallas_call(
        sum_kernel,
        out_shape=[jax.ShapeDtypeStruct((5, 8, 128), F32)] * 2,
        compiler_params=pltpu.CompilerParams(vmem_limit_bytes=MUCH_VMEM),
        cost_estimate=pl.CostEstimate(flops=10**6, bytes_accessed=1 << 20, transcendentals=0),
        name="sum_shares",
    )(shares)


def core_kernel(crossed_hbm, lat_ref, send_ref, keep_ref, lat_core, crossed, arrived):
    def crossed_copy(owner):
        part = pl.ds(owner * 12, 12)
        return pltpu.make_async_copy(crossed_hbm.at[part], crossed.at[part], arrived.at[owner])

    for owner in range(8):
        crossed_copy(owner).start()
    lat_core[:96] = lat_ref[...]
    lat_core[96:] = jnp.zeros((16, 128), F32)

    core = lax.axis_index("lat") % 2
    of_core = [
        jnp.concatenate([lat_core[pl.ds(at * 6 + b, 8, stride=12), :] for b in range(6)], axis=0) for at in range(2)
    ]
    lat_rows = jnp.concatenate(
        [jnp.where(core == 0, of_core[0], of_core[1]), jnp.where(core == 0, of_core[1], of_core[0])], axis=0
    )
    lat_top, lat_low = halves(lat_rows)
    lats = jnp.concatenate(
        [jnp.concatenate([lat_top, lat_top], axis=1), jnp.concatenate([lat_low, jnp.zeros_like(lat_low)], axis=1)],
        axis=0,
    )

    def share(owner, carry):
        crossed_copy(owner).wait()
        block = crossed[pl.ds(owner * 12, 12)].reshape(960, 128)
        block = jnp.concatenate([block, jnp.zeros((64, 128), F32)], axis=0)
        result = dot(lats, jnp.concatenate(halves(block), axis=1), ((1,), (1,)))
        result = result[:96] + result[96:]
        for part, out in enumerate((keep_ref, send_ref)):
            for b in range(6):
                row = part * 48 + b * 8
                for q in range(8):
                    out[owner, :, q * 6 + b, :] = result[row : row + 8, q * 128 : q * 128 + 128]
        return carry

    lax.fori_loop(0, 8, share, 0)


def core_partials(crossed, lat_core):
    part = jax.ShapeDtypeStruct((8, 8, 48, 128), F32)
    return pl.pallas_call(
        core_kernel,
        in_specs=[pl.BlockSpec(memory_space=pl.ANY)] + in_vmem(1),
        out_specs=in_vmem(2),
        out_shape=[part, part],
        scratch_shapes=[
            pltpu.VMEM((112, 128), F32),
            pltpu.VMEM(crossed.shape, F32),
            pltpu.SemaphoreType.DMA((8,)),
        ],
        compiler_params=pltpu.CompilerParams(vmem_limit_bytes=MORE_VMEM),
        cost_estimate=pl.CostEstimate(flops=20 * 10**9, bytes_accessed=8 << 20, transcendentals=0),
        name="core_partials",
    )(crossed, lat_core)


def join_kernel(keep_ref, arrived_ref, mine_ref, other_ref, out_hbm, out, sums, sent):
    sums[...] = mine_ref[...] + other_ref[...]
    copies = []
    for slot, chip in enumerate(SLOTS):
        lat = chip % 8
        row = lat % 2 * 4
        out[slot, :48] = keep_ref[chip] + arrived_ref[chip]
        out[slot, 48:52] = sums[lat // 2, row : row + 4]
        out[slot, 52:] = sums[4, :4]
        if slot % 8 == 7:
            piece = pl.ds(slot - 7, 8)
            copies.append(pltpu.make_async_copy(out.at[piece], out_hbm.at[piece], sent.at[slot // 8]))
            copies[-1].start()
    for copy in copies:
        copy.wait()


def join_shares(keep, arrived, mine, other):
    shape = (64, 56, 128)
    return pl.pallas_call(
        join_kernel,
        in_specs=in_vmem(4),
        out_specs=pl.BlockSpec(memory_space=pl.ANY),
        out_shape=jax.ShapeDtypeStruct(shape, F32),
        scratch_shapes=[pltpu.VMEM(shape, F32), pltpu.VMEM(mine.shape, F32), pltpu.SemaphoreType.DMA((8,))],
        compiler_params=pltpu.CompilerParams(vmem_limit_bytes=MORE_VMEM),
        cost_estimate=pl.CostEstimate(flops=10**6, bytes_accessed=5 << 20, transcendentals=0),
        name="join_shares",
    )(keep, arrived, mine, other)


def lon_kernel(field_hbm, lat_ref, time_ref, keep_ref, send_ref, field, arrived, lat_test, total):
    start_field(field_hbm, field, arrived, range(2))
    total[...] = jnp.zeros_like(total)
    lat_test[...] = lat_ref[...].T
    lons = total.shape[0]

    def work(at):
        times = time_ref[pl.ds(at * HOURS, HOURS), :]
        tests = [lat_test[...] * times[hour : hour + 1, :] for hour in range(HOURS)]
        test_top, test_low = halves(jnp.concatenate(tests, axis=0))
        values = [halves(field[at * HOURS + hour]) for hour in range(HOURS)]
        top = jnp.concatenate([value[0] for value in values], axis=1)
        low = jnp.concatenate([value[1] for value in values], axis=1)
        upper = dot(jnp.concatenate([top, low], axis=0), test_top)
        total[...] += upper[:lons] + upper[lons:] + dot(top, test_low)

    each_block(field_hbm, field, arrived, work)
    place = lax.axis_index("lat")
    core, z, x_lo = place % 2, place // 2 % 4, place // 8
    for step in range(4):
        for flip in range(2):
            x = x_lo + flip - 2 * x_lo * flip
            owner = x * 8 + (z + step) % 4 * 2
            for out, of_core in ((keep_ref, core), (send_ref, 1 - core)):
                out[step, flip] = total[pl.ds(pl.multiple_of((owner + of_core) * 32, 32), 32), :]


def lon_partial(field, lat_test_t, time_test):
    hours, lons, lats = field.shape
    rank = lat_test_t.shape[0]
    out = jax.ShapeDtypeStruct((4, 2, 32, rank), F32)
    return pl.pallas_call(
        lon_kernel,
        in_specs=in_hbm(1) + in_vmem(2),
        out_specs=in_vmem(2),
        out_shape=[out, out],
        scratch_shapes=field_scratch(hours, lons, lats)
        + [pltpu.VMEM((lats, rank), F32), pltpu.VMEM((lons, rank), F32)],
        compiler_params=pltpu.CompilerParams(vmem_limit_bytes=MUCH_VMEM),
        cost_estimate=pl.CostEstimate(flops=12 * 10**9, bytes_accessed=22 << 20, transcendentals=0),
        name="lon_partial",
    )(field, lat_test_t, time_test)


def finish_kernel(parts_ref, time_ref, core_ref, lat_ref, hour_ref, columns):
    total = parts_ref[0, :48]
    for source in range(1, parts_ref.shape[0]):
        total = total + parts_ref[source, :48]
    modes = [jnp.concatenate([total[q * 6 : q * 6 + 6], jnp.zeros((2, 128), F32)], axis=0) for q in range(8)]
    modes = jnp.concatenate(modes, axis=1)
    rows = jnp.concatenate([modes[:, a * 80 : a * 80 + 80] for a in range(12)], axis=0)
    result = lax.dot_general(
        rows,
        time_ref[...],
        (((1,), (0,)), ((), ())),
        precision=lax.Precision.HIGHEST,
        preferred_element_type=F32,
    )
    for a in range(12):
        core_ref[a] = result[a * 8 : a * 8 + 6]
    for slot, chip in enumerate(SLOTS):
        if chip < 50:
            lat_ref[chip * 4 : chip * 4 + 4] = parts_ref[slot, 48:52]
            columns[chip * 4 : chip * 4 + 4] = parts_ref[slot, 52:]
    hour_ref[...] = columns[...].T[:80]


def finish(parts, time_core_t):
    return pl.pallas_call(
        finish_kernel,
        out_shape=[
            jax.ShapeDtypeStruct((12, 6, 96), F32),
            jax.ShapeDtypeStruct((200, 128), F32),
            jax.ShapeDtypeStruct((80, 200), F32),
        ],
        scratch_shapes=[pltpu.VMEM((200, 128), F32)],
        compiler_params=pltpu.CompilerParams(vmem_limit_bytes=VMEM),
        cost_estimate=pl.CostEstimate(flops=10**8, bytes_accessed=2 << 20, transcendentals=0),
        name="finish",
    )(parts, time_core_t)


def places(move):
    pairs = []
    for source in range(128):
        lon, lat = divmod(source, 16)
        x, y, z, core = (lon % 2) * 2 + lat // 8, lon // 2, lat // 2 % 4, lat % 2
        x, y, z, core = move(x, y, z, core)
        pairs.append((source, (y * 2 + x // 2) * 16 + x % 2 * 8 + z * 2 + core))
    return pairs


OTHER_CORE = places(lambda x, y, z, core: (x, y, z, 1 - core))
Z_STEPS = [places(lambda x, y, z, core: (x, y, (z + step) % 4, core)) for step in range(4)]
X_FLIP = places(lambda x, y, z, core: (x ^ 1, y, z, core))
CHIPS = [[chip // 8 * 16 + chip % 8 * 2 + core for chip in SLOTS] for core in (0, 1)]


def on_device(field, lon_test, lat_test, time_test, lon_core, lat_core, time_core):
    crossed, sums = first_partials(field, lon_core, lon_test.T, lat_test.T, time_test)

    shares = lax.all_to_all(sums, BOTH, 0, 0)
    send, keep = core_partials(crossed, lat_core)
    shares, send, keep = lax.optimization_barrier((shares, send, keep))
    other = lax.ppermute(send, BOTH, OTHER_CORE)
    mine, others = sum_shares(shares)
    others = lax.ppermute(others, BOTH, OTHER_CORE)

    chip = join_shares(keep.reshape(64, 48, 128), other.reshape(64, 48, 128), mine, others)
    parts = lax.all_to_all(chip, BOTH, 0, 0, axis_index_groups=CHIPS)

    field, _ = lax.optimization_barrier((field, chip))
    keep, send = lon_partial(field, lat_test.T, time_test)
    rows = keep + lax.ppermute(send, BOTH, OTHER_CORE)
    total = rows[0]
    for step in range(1, 4):
        total = total + lax.ppermute(rows[step], BOTH, Z_STEPS[step])
    total, parts = lax.optimization_barrier((total, parts))
    sketch_lon = total[0] + lax.ppermute(total[1], BOTH, X_FLIP)

    core_sketch, sketch_lat, sketch_time = finish(parts, time_core.T)
    return (sketch_lon, sketch_lat.T, sketch_time, core_sketch.transpose(2, 0, 1))


def solution(mesh):
    return jax.shard_map(
        on_device,
        mesh=mesh,
        in_specs=(
            P(None, "lon", "lat"),
            P("lon", None),
            P("lat", None),
            P(),
            P(None, "lon"),
            P(None, "lat"),
            P(),
        ),
        out_specs=(P(("lon", "lat"), None), P("lat", None), P(), P(None, "lon", "lat")),
        check_vma=False,
    )
```
